512 devices in a mesh: pipe: 4 (over z_lo), expert: 64 (over y, x, core), dp: 2 (over z_hi).
Axes of the slice: x: 4, y: 8, z: 8 (z_hi: 2, z_lo: 4; z = z_hi * 4 + z_lo), core: 2. Of those that a mesh axis runs over, the one named last changes fastest.
Arguments:
- section_inputs: bfloat16 [4, 4096, 2048], P('pipe', ('expert', 'dp')), may hold values from -6 to 6
- saved_inputs: bfloat16 [4, 4096, 2048], P('pipe', ('expert', 'dp')), may hold values from -6 to 6
- output_grads: bfloat16 [4, 4096, 2048], P('pipe', ('expert', 'dp')), may hold values from -6 to 6
- forward_routes: int32 [4, 4096, 8], P('pipe', ('expert', 'dp')), may hold values from 0 to 63, as said below
- backward_routes: int32 [4, 4096, 8], P('pipe', ('expert', 'dp')), may hold values from 0 to 63, as said below
- forward_gates: float32 [4, 4096, 8], P('pipe', ('expert', 'dp')), may hold values from 0.1 to 0.9
- backward_gates: float32 [4, 4096, 8], P('pipe', ('expert', 'dp')), may hold values from 0.1 to 0.9
- expert_weights: bfloat16 [4, 64, 2048, 768], P('pipe', 'expert'), may hold values from -0.125 to 0.125
Outputs:
- next_inputs: bfloat16 [4, 4096, 2048], P('pipe', ('expert', 'dp'))
- prior_grads: bfloat16 [4, 4096, 2048], P('pipe', ('expert', 'dp'))
- weight_grads: bfloat16 [4, 64, 2048, 768], P('pipe', 'expert', 'dp')
The draws below stay inside these ranges and needn't reach their ends.
Inputs may be any that keep to these rules, and one draw needn't show every extreme that they name: `forward_routes`: each token names 8 different experts. Among the tokens of one aligned block of 32 (the tokens of one device) no expert is named more than 5 times, and in each section one expert is named exactly 5 times in every block. `backward_routes`: as for forward_routes.
All inputs are finite; a program needn't handle non-finite values.
Results may differ from the reference program's by a relative error of at most 0.012.
Values may be sent and summed in bfloat16 or wider, within the bound.
A program may use at most 64 MiB of HBM per device.

```python
import jax
import jax.numpy as jnp

D = 2048
HID = 768
EXPERTS = 64
TOP = 8
TOK_DEV = 32
SECTIONS = 4
TOKENS = 4096
CAP = 5
N_DP = 2


def block_route(key, hottest):
    order_key, crowd_key, token_key, column_key = jax.random.split(key, 4)
    labels = jnp.arange(EXPERTS, dtype=jnp.int32)
    ranking = jnp.argsort(jax.random.permutation(order_key, EXPERTS)).astype(jnp.int32)
    hot_rank = ranking[hottest]
    ranking = jnp.where(labels == hottest, 0, jnp.where(ranking < hot_rank, ranking + 1, ranking)).astype(jnp.int32)
    crowded = jax.random.randint(crowd_key, (), 1, EXPERTS // 8 + 1, dtype=jnp.int32)
    leftover = TOK_DEV * TOP - crowded * CAP
    spread = EXPERTS - crowded
    base_count = leftover // spread
    extra_count = leftover - base_count * spread
    by_rank = jnp.where(labels < crowded, CAP, jnp.where(labels - crowded < extra_count, base_count + 1, base_count)).astype(jnp.int32)
    counts = by_rank[ranking]
    listed = jnp.repeat(labels, counts, total_repeat_length=TOK_DEV * TOP)
    dealt_ids = listed.reshape(TOP, TOK_DEV).T
    dealt_ids = dealt_ids[jax.random.permutation(token_key, TOK_DEV)]
    column_keys = jax.random.split(column_key, TOK_DEV)
    return jax.vmap(jax.random.permutation)(column_keys, dealt_ids).astype(jnp.int32)


def section_routes(key):
    blocks = TOKENS // TOK_DEV
    hot_key, block_key = jax.random.split(key)
    hottest = jax.random.randint(hot_key, (), 0, EXPERTS, dtype=jnp.int32)
    block_keys = jax.random.split(block_key, blocks)

    def one_block(single_key):
        return block_route(single_key, hottest)
    return jax.vmap(one_block)(block_keys).reshape(TOKENS, TOP)


def route_table(key):
    section_keys = jax.random.split(key, SECTIONS)
    return jax.vmap(section_routes)(section_keys)


def draw_forward_routes(key, part):
    return route_table(jax.random.fold_in(key, 11))


def draw_backward_routes(key, part):
    return route_table(jax.random.fold_in(key, 23))


def shard_levels(own_key, shape, cuts, least, high):
    loudness, own = 1.0, jax.random.fold_in(own_key, 6)
    for dim, blocks in cuts:
        heights = jnp.exp(jax.random.uniform(jax.random.fold_in(own, dim), (blocks,), jnp.float32, least / len(cuts), high / len(cuts)))
        loudness = loudness * jnp.repeat(heights, shape[dim] // blocks).reshape([-1 if axis == dim else 1 for axis in range(len(shape))])
    return loudness


def scatter_about(own_key, extent, width, bound, cuts=(), kind=jnp.bfloat16):
    array = jax.random.normal(own_key, extent, jnp.float32) * width
    if len(cuts) > 0:
        array = shard_levels(own_key, extent, cuts, -0.22, 0.18) * array
    return jnp.clip(array, min=-bound, max=bound).astype(kind)


def setup_inputs(seed: int = 0) -> dict:
    keys = jax.random.split(jax.random.key(seed), 9)
    section_inputs = scatter_about(keys[0], (SECTIONS, TOKENS, D), 1.0, 6.0, ((0, 4), (1, 128)))
    saved_inputs = scatter_about(keys[1], (SECTIONS, TOKENS, D), 1.0, 6.0, ((0, 4), (1, 128)))
    output_grads = scatter_about(keys[2], (SECTIONS, TOKENS, D), 1.0, 6.0, ((0, 4), (1, 128)))
    forward_routes = draw_forward_routes(jax.random.fold_in(keys[8], 71), 0)
    backward_routes = draw_backward_routes(jax.random.fold_in(keys[8], 71), 0)
    forward_gates = jnp.clip(0.1 + 0.79999997 * jax.random.uniform(keys[5], (SECTIONS, TOKENS, TOP), jnp.float32) ** shard_levels(keys[5], (SECTIONS, TOKENS, TOP), ((0, 4), (1, 128)), -0.2, 0.2), 0.1, 0.9)
    backward_gates = jnp.clip(0.1 + 0.79999997 * jax.random.uniform(keys[6], (SECTIONS, TOKENS, TOP), jnp.float32) ** shard_levels(keys[6], (SECTIONS, TOKENS, TOP), ((0, 4), (1, 128)), -0.2, 0.2), 0.1, 0.9)
    expert_weights = scatter_about(keys[7], (SECTIONS, EXPERTS, D, HID), D ** -0.5, 0.125, ((0, 4), (1, 64)))
    return {"section_inputs": section_inputs, "saved_inputs": saved_inputs, "output_grads": output_grads, "forward_routes": forward_routes, "backward_routes": backward_routes, "forward_gates": forward_gates, "backward_gates": backward_gates, "expert_weights": expert_weights}


def slot_index(routing, experts, capacity):
    one_hot = (routing[..., None] == jnp.arange(experts, dtype=jnp.int32)).astype(jnp.int32)
    before = jnp.cumsum(one_hot, axis=-2) - one_hot
    return (routing * capacity + jnp.sum(before * one_hot, axis=-1)).astype(jnp.int32)


def pack_rows(source, slot_ids, slot_total, spread):
    row_count = slot_ids.shape[0]
    owner_row = jnp.zeros((slot_total,), jnp.int32).at[slot_ids].set(jnp.arange(row_count, dtype=jnp.int32) + 1)
    filled = owner_row > 0
    picked = jnp.take(source, (jnp.maximum(owner_row - 1, 0) // spread).astype(jnp.int32), axis=0)
    return jnp.where(filled[:, None], picked, jnp.zeros_like(picked))


def gather_slots(table, slot_ids):
    return jnp.take(table, slot_ids, axis=0)


def silu_slope(hidden):
    sigma = jax.nn.sigmoid(hidden)
    return sigma * (1.0 + hidden * (1.0 - sigma))


def reference(section_inputs, saved_inputs, output_grads, forward_routes, backward_routes, forward_gates, backward_gates, expert_weights):
    blocks = TOKENS // TOK_DEV
    row_total = TOK_DEV * TOP
    slot_total = EXPERTS * CAP
    halves = blocks // N_DP
    packer = jax.vmap(pack_rows, in_axes=(0, 0, None, None))
    picker = jax.vmap(gather_slots)
    layer_list = []
    grad_list = []
    weight_list = []
    for section_id in range(SECTIONS):
        weights = expert_weights[section_id].astype(jnp.float32)
        inputs = section_inputs[section_id].reshape(blocks, TOK_DEV, D)
        forward_slot = slot_index(forward_routes[section_id].reshape(blocks, row_total), EXPERTS, CAP)
        slot_rows = packer(inputs, forward_slot, slot_total, TOP).reshape(blocks, EXPERTS, CAP, D)
        hidden = jnp.einsum('becd,edf->becf', slot_rows.astype(jnp.float32), weights)
        active = jax.nn.silu(hidden).astype(jnp.bfloat16)
        result = jnp.einsum('becf,edf->becd', active.astype(jnp.float32), weights).astype(jnp.bfloat16)
        picked = picker(result.reshape(blocks, slot_total, D), forward_slot).reshape(blocks, TOK_DEV, TOP, D)
        gate_values = forward_gates[section_id].reshape(blocks, TOK_DEV, TOP, 1)
        layer_out = inputs.astype(jnp.float32) + jnp.sum(gate_values * picked.astype(jnp.float32), axis=2)
        layer_list.append(layer_out.astype(jnp.bfloat16).reshape(TOKENS, D))

        saved_block = saved_inputs[section_id].reshape(blocks, TOK_DEV, D)
        grad_block = output_grads[section_id].reshape(blocks, TOK_DEV, D)
        backward_slot = slot_index(backward_routes[section_id].reshape(blocks, row_total), EXPERTS, CAP)
        saved_rows = packer(saved_block, backward_slot, slot_total, TOP).reshape(blocks, EXPERTS, CAP, D)
        scaled = backward_gates[section_id].reshape(blocks, TOK_DEV, TOP, 1) * grad_block.astype(jnp.float32)[:, :, None, :]
        scaled = scaled.astype(jnp.bfloat16).reshape(blocks, row_total, D)
        slot_grads = packer(scaled, backward_slot, slot_total, 1).reshape(blocks, EXPERTS, CAP, D)
        back_hidden = jnp.einsum('becd,edf->becf', saved_rows.astype(jnp.float32), weights)
        back_active = jax.nn.silu(back_hidden).astype(jnp.bfloat16)
        active_grads = jnp.einsum('becd,edf->becf', slot_grads.astype(jnp.float32), weights)
        hidden_grads = (active_grads * silu_slope(back_hidden)).astype(jnp.bfloat16)
        row_grads = jnp.einsum('becf,edf->becd', hidden_grads.astype(jnp.float32), weights).astype(jnp.bfloat16)
        picked_grads = picker(row_grads.reshape(blocks, slot_total, D), backward_slot).reshape(blocks, TOK_DEV, TOP, D)
        input_grads = grad_block.astype(jnp.float32) + jnp.sum(picked_grads.astype(jnp.float32), axis=2)
        grad_list.append(input_grads.astype(jnp.bfloat16).reshape(TOKENS, D))

        saved_split = saved_rows.reshape(halves, N_DP, EXPERTS, CAP, D).astype(jnp.float32)
        hidden_split = hidden_grads.reshape(halves, N_DP, EXPERTS, CAP, HID).astype(jnp.float32)
        slot_split = slot_grads.reshape(halves, N_DP, EXPERTS, CAP, D).astype(jnp.float32)
        active_split = back_active.reshape(halves, N_DP, EXPERTS, CAP, HID).astype(jnp.float32)
        half_grads = jnp.einsum('bgecd,bgecf->gedf', saved_split, hidden_split) + jnp.einsum('bgecd,bgecf->gedf', slot_split, active_split)
        half_grads = half_grads.astype(jnp.bfloat16)
        weight_list.append(jnp.sum(half_grads.astype(jnp.float32), axis=0).astype(jnp.bfloat16))
    next_inputs = jnp.roll(jnp.stack(layer_list), 1, axis=0)
    prior_grads = jnp.roll(jnp.stack(grad_list), -1, axis=0)
    return next_inputs, prior_grads, jnp.stack(weight_list)
```

```python
import functools

import jax
import jax.numpy as jnp
from jax import lax
from jax.experimental import pallas as pl
from jax.experimental.pallas import tpu as pltpu
from jax.sharding import PartitionSpec as P

MESH = pl.DeviceIdType.MESH
BF = jnp.bfloat16
F32 = jnp.float32
TOK = 32
CAP = 5
NY = 8
NQ = 8
WIDE = 1024
SLOT = NY * CAP
D = 2048
HID = 768
PIECES = 4


def dot(a, b):
    return jnp.dot(a, b, preferred_element_type=F32)


def dot_t(a, b):
    return lax.dot_general(a, b, (((1,), (1,)), ((), ())), preferred_element_type=F32)


def dot_tl(a, b):
    return lax.dot_general(a, b, (((0,), (0,)), ((), ())), preferred_element_type=F32)


def tile(i, n):
    return pl.ds(pl.multiple_of(i * n, n), n)


def kernel(
    meta_ref, s_ref, o_ref, f_ref, w_hbm,
    next_ref, prior_ref, wg_ref,
    w, metas, xbuf, xsend, xrecv, rsend, rrecv, ha, pair, hgf, frow, fh, pack, gcol, comb, part,
    ysend, yrecv, out_send, out_recv, wsend, wrecv,
    w_sem, ms, mr, gs, gr, xs, xr, bs, br, ys, yr, ds_, dr, ps, pr,
):
    e = lax.axis_index("expert")
    p = lax.axis_index("pipe")
    half = lax.axis_index("dp")
    y, q = e // NQ, e % NQ
    x, c = q // 2, q % 2

    def ydev(k):
        return {"expert": ((y + k + NY) % NY) * NQ + q}

    def qdev(j):
        jx, jc = j // 2, j % 2
        other = ((x // 2 + jx // 2) % 2) * 2 + (x % 2 + jx % 2) % 2
        return {"expert": y * NQ + other * 2 + (c + jc) % 2}

    def send(src, dst, ssem, rsem, dev):
        return pltpu.make_async_remote_copy(
            src_ref=src, dst_ref=dst, send_sem=ssem, recv_sem=rsem, device_id=dev, device_id_type=MESH
        )

    sent = []

    def start(copy):
        copy.start()
        sent.append(copy)
        return copy

    w_copy = pltpu.make_async_copy(w_hbm, w, w_sem)
    w_copy.start()

    for i in range(2):
        cols = pl.ds(i * WIDE, WIDE)
        xbuf[i, 0, 0:TOK, :] = s_ref[:, cols]
        xbuf[i, 0, TOK : 2 * TOK, :] = o_ref[:, cols]
        xbuf[2, 0, i * TOK : (i + 1) * TOK, :] = f_ref[:, cols]
    metas[0] = meta_ref[...]

    barrier = pltpu.get_barrier_semaphore()
    friends = [ydev(k) for k in range(1, NY)] + [qdev(j) for j in range(1, NQ)]
    friends += [{"dp": 1 - half}, {"pipe": (p + 1) % 4}, {"pipe": (p + 3) % 4}]
    for dev in friends:
        pl.semaphore_signal(barrier, inc=1, device_id=dev, device_id_type=MESH)
    pl.semaphore_wait(barrier, len(friends))

    def gather(i, step):
        ups, downs = (NY - step + 1) % NY, step - 1
        upd, downd = (NY - step) % NY, step
        if step < 4:
            rows = (slice(None), slice(None))
        else:
            rows = (pl.ds(0, TOK), pl.ds(TOK, TOK))
        up = send(xbuf.at[i, ups, rows[0]] if step == 4 else xbuf.at[i, ups],
                  xbuf.at[i, upd, rows[0]] if step == 4 else xbuf.at[i, upd],
                  gs.at[i, step - 1, 0], gr.at[i, step - 1, 0], ydev(1))
        down = send(xbuf.at[i, downs, rows[1]] if step == 4 else xbuf.at[i, downs],
                    xbuf.at[i, downd, rows[1]] if step == 4 else xbuf.at[i, downd],
                    gs.at[i, step - 1, 1], gr.at[i, step - 1, 1], ydev(-1))
        return start(up), start(down)

    def arrive(pairs):
        for copy in pairs:
            copy.wait_recv()

    g = {}
    g[0] = gather(0, 1)
    meta_copies = [
        start(send(metas.at[0], metas.at[NY - k], ms.at[k], mr.at[NY - k], ydev(k))) for k in (1, 7, 2, 6, 3, 5, 4)
    ]
    g[1] = gather(1, 1)

    def forward(i, step):
        arrive(g[i])
        g[i] = gather(i, step)

    forward(0, 2)
    forward(1, 2)
    g[2] = gather(2, 1)

    for k in range(1, NY):
        send(metas.at[0], metas.at[k], ms.at[k], mr.at[k], ydev(k)).wait_recv()
    lane = lax.broadcasted_iota(jnp.int32, (4 * NQ, 128), 1) // TOK
    parts = []
    for h in range(2):
        v = metas[4 * h]
        for k in range(1, 4):
            v = jnp.where(lane == k, metas[4 * h + k], v)
        parts.append(v)
    table = jnp.concatenate(parts, axis=1)
    wide = NY * TOK
    jrow = lax.broadcasted_iota(jnp.int32, (NQ, wide), 0)
    expert = (y * NQ + jnp.bitwise_xor(jrow, q)).astype(F32)
    marks, gates = [], []
    for t in range(2):
        mark = jnp.zeros((NQ, wide), F32)
        gate = jnp.zeros((NQ, wide), F32)
        for k in range(8):
            same = table[t * 8 + k : t * 8 + k + 1, :] == expert
            mark = mark + jnp.where(same, 1.0, 0.0)
            gate = gate + jnp.where(same, table[16 + t * 8 + k : 17 + t * 8 + k, :], 0.0)
        marks.append(mark)
        gates.append(gate)
    r2 = lax.broadcasted_iota(jnp.int32, (wide, wide), 0)
    l2 = lax.broadcasted_iota(jnp.int32, (wide, wide), 1)
    earlier = jnp.where((r2 // TOK == l2 // TOK) & (r2 < l2), 1.0, 0.0).astype(BF)
    both = jnp.concatenate(marks, axis=0)
    before = dot(both.astype(BF), earlier)
    place = jnp.where(both > 0.5, before, -1.0)
    rr = lax.broadcasted_iota(jnp.int32, (SLOT, wide), 0)
    ll = lax.broadcasted_iota(jnp.int32, (SLOT, wide), 1)
    block = lax.shift_right_logical(rr * 52, 8)
    want = jnp.where(ll // TOK == block, rr - block * CAP, -2).astype(F32)
    zeros = jnp.zeros((SLOT, wide), F32)
    for t in range(2):
        ones, lefts, rights, cols = [], [], [], []
        for j in range(NQ):
            row = t * NQ + j
            hit = jnp.where(place[row : row + 1, :] == want, 1.0, 0.0)
            gated = hit * gates[t][j : j + 1, :]
            ones.append(hit)
            weight = gated if t == 0 else hit
            lefts += [weight, zeros]
            rights += [zeros, weight]
            if t == 1:
                cols.append(jnp.sum(gated, axis=1, keepdims=True))
        pack[t] = jnp.concatenate(ones, axis=0).astype(BF)
        if t == 1:
            gcol[...] = jnp.broadcast_to(jnp.concatenate(cols, axis=0), gcol.shape)
        comb[t, 0] = jnp.concatenate(lefts, axis=0).T.astype(BF)
        comb[t, 1] = jnp.concatenate(rights, axis=0).T.astype(BF)

    forward(0, 3)
    forward(1, 3)
    forward(0, 4)
    forward(1, 4)

    ORDER = (4, 5, 2, 3, 6, 7, 1)

    def exchange(i, t):
        @pl.loop(0, WIDE // 256)
        def _(n):
            at = tile(n, 256)
            top = dot(pack[t], xbuf[i, :, 0:TOK, at].reshape(wide, 256))
            low = dot(pack[t], xbuf[i, :, TOK : 2 * TOK, at].reshape(wide, 256))
            if t == 1:
                low = low * gcol[:, 0:1]
            for j in range(NQ):
                rows = slice(j * SLOT, (j + 1) * SLOT)
                msg = jnp.concatenate([top[rows], low[rows]], axis=0).astype(BF)
                if j == 0:
                    xrecv[i, 0, :, at] = msg
                else:
                    xsend[i, j, :, at] = msg

        return [start(send(xsend.at[i, j], xrecv.at[i, j], xs.at[i, j], xr.at[i, j], qdev(j))) for j in ORDER]

    arrive(g[0])
    x0 = exchange(0, 1)
    forward(2, 2)
    arrive(g[1])
    x1 = exchange(1, 1)
    forward(2, 3)
    w_copy.wait()

    def accumulate(i, first):
        @pl.loop(0, HID // 256)
        def _(n):
            at = tile(n, 256)
            v = dot(xrecv[i].reshape(2 * SLOT * NQ, WIDE), w[pl.ds(i * WIDE, WIDE), at])
            ha[:, at] = v if first else ha[:, at] + v

    arrive(x0)
    accumulate(0, True)
    forward(2, 4)
    arrive(g[2])
    arrive(x1)
    x2 = exchange(2, 0)
    accumulate(1, False)

    @pl.loop(0, NQ)
    def _(j):
        h = ha[pl.ds(pl.multiple_of(j * 2 * SLOT, 8), SLOT), :]
        a = ha[pl.ds(pl.multiple_of(j * 2 * SLOT + SLOT, 8), SLOT), :]
        s = jax.nn.sigmoid(h)
        hg = a * s * (1.0 + h * (1.0 - s))
        pair[pl.ds(pl.multiple_of(j * 2 * SLOT, 16), 2 * SLOT), :] = jnp.concatenate([hg, h * s], axis=0).astype(BF)
        hgf[pl.ds(pl.multiple_of(j * SLOT, 8), SLOT), :] = hg

    per = WIDE // PIECES
    wcopies = []
    for k in range(PIECES):
        rows = xrecv[1 - half, :, :, k * per : (k + 1) * per].reshape(2 * SLOT * NQ, per)
        wsend[k] = dot_tl(rows, pair[...]).astype(BF)
        wcopies.append(start(send(wsend.at[k], wrecv.at[k], ds_.at[k], dr.at[k], {"dp": 1 - half})))

    def give_back(t, rows):
        @pl.loop(0, WIDE // 256)
        def _(n):
            at = tile(n, 256)
            left = dot_t(rows, w[tile(n, 256), :])
            right = dot_t(rows, w[pl.ds(pl.multiple_of(WIDE + n * 256, 256), 256), :])
            for j in range(NQ):
                cut = slice(j * SLOT, (j + 1) * SLOT)
                msg = jnp.concatenate([left[cut], right[cut]], axis=0).astype(BF)
                if j == 0:
                    rrecv[t, 0, :, at] = msg
                else:
                    rsend[t, j, :, at] = msg

        return [start(send(rsend.at[t, j], rrecv.at[t, j], bs.at[t, j], br.at[t, j], qdev(j))) for j in ORDER]

    b1 = give_back(1, hgf[...].astype(BF))

    for k in range(PIECES):
        rows = xrecv[half, :, :, k * per : (k + 1) * per].reshape(2 * SLOT * NQ, per)
        wg_ref[k * per : (k + 1) * per, :] = dot_tl(rows, pair[...]).astype(BF)

    arrive(x2)

    @pl.loop(0, WIDE // 256)
    def _(n):
        v = xrecv[2, :, :, tile(n, 256)].astype(F32)
        frow[:, tile(n, 256)] = v[:, 0:SLOT].reshape(SLOT * NQ, 256).astype(BF)
        frow[:, pl.ds(pl.multiple_of(WIDE + n * 256, 256), 256)] = v[:, SLOT:].reshape(SLOT * NQ, 256).astype(BF)

    @pl.loop(0, HID // 256)
    def _(n):
        h = dot(frow[...], w[:, tile(n, 256)])
        fh[:, tile(n, 256)] = (h * jax.nn.sigmoid(h)).astype(BF)

    b0 = give_back(0, fh[...])

    def combine(t):
        @pl.loop(0, WIDE // 256)
        def _(n):
            at = tile(n, 256)
            rows = rrecv[t, :, :, at].reshape(2 * SLOT * NQ, 256)
            part[t, :, 0:TOK, at] = dot(comb[t, 0], rows).reshape(NY, TOK, 256)
            part[t, :, TOK : 2 * TOK, at] = dot(comb[t, 1], rows).reshape(NY, TOK, 256)

    r = {}

    def reduce_step(t, step):
        if step == 1:
            ysend[t, 0, 0, 0:TOK] = part[t, 4, 0:TOK].astype(BF)
            ysend[t, 0, 1, TOK : 2 * TOK] = part[t, 4, TOK : 2 * TOK].astype(BF)
            refs = [
                (ysend.at[t, 0, 0, pl.ds(0, TOK)], yrecv.at[t, 0, 0, pl.ds(0, TOK)]),
                (ysend.at[t, 0, 1, pl.ds(TOK, TOK)], yrecv.at[t, 0, 1, pl.ds(TOK, TOK)]),
            ]
        else:
            s = step - 1
            for way in range(2):
                r[t][way].wait_recv()
                d = 5 - step if way == 0 else 3 + step
                if step == 2:
                    got = slice(0, TOK) if way == 0 else slice(TOK, 2 * TOK)
                    rest = slice(TOK, 2 * TOK) if way == 0 else slice(0, TOK)
                    ysend[t, s, way, got] = (part[t, d, got] + yrecv[t, 0, way, got].astype(F32)).astype(BF)
                    ysend[t, s, way, rest] = part[t, d, rest].astype(BF)
                else:
                    ysend[t, s, way] = (part[t, d] + yrecv[t, s - 1, way].astype(F32)).astype(BF)
            refs = [(ysend.at[t, s, way], yrecv.at[t, s, way]) for way in range(2)]
        r[t] = [
            start(send(*refs[way], ys.at[t, step - 1, way], yr.at[t, step - 1, way], ydev(1 - 2 * way)))
            for way in range(2)
        ]

    def finish(t, base_ref, to):
        arrive(r[t])
        total = part[t, 0] + yrecv[t, 3, 0].astype(F32) + yrecv[t, 3, 1].astype(F32)
        out_send[t, :, 0:WIDE] = (base_ref[:, 0:WIDE].astype(F32) + total[0:TOK]).astype(BF)
        out_send[t, :, WIDE:] = (base_ref[:, WIDE:].astype(F32) + total[TOK:]).astype(BF)
        return start(send(out_send.at[t], out_recv.at[t], ps.at[t], pr.at[t], {"pipe": to}))

    arrive(b1)
    combine(1)
    for step in range(1, 5):
        reduce_step(1, step)
    arrive(b0)
    combine(0)
    reduce_step(0, 1)
    prior = finish(1, o_ref, (p + 3) % 4)
    for step in range(2, 5):
        reduce_step(0, step)
    after = finish(0, f_ref, (p + 1) % 4)
    for k in range(PIECES):
        wcopies[k].wait_recv()
        at = slice(k * per, (k + 1) * per)
        wg_ref[at, :] = (wg_ref[at, :].astype(F32) + wrecv[k].astype(F32)).astype(BF)
    prior.wait_recv()
    prior_ref[...] = out_recv[1]
    after.wait_recv()
    next_ref[...] = out_recv[0]
    for copy in sent:
        copy.wait_send()


def relay(meta, s, o, f, w):
    vmem = pl.BlockSpec(memory_space=pltpu.VMEM)
    dma = pltpu.SemaphoreType.DMA
    v = pltpu.VMEM
    two = 2 * SLOT
    return pl.pallas_call(
        kernel,
        out_shape=(
            jax.ShapeDtypeStruct((TOK, D), BF),
            jax.ShapeDtypeStruct((TOK, D), BF),
            jax.ShapeDtypeStruct((D // 2, HID), BF),
        ),
        in_specs=[vmem, vmem, vmem, vmem, pl.BlockSpec(memory_space=pl.ANY)],
        out_specs=(vmem, vmem, vmem),
        scratch_shapes=[
            v((D, HID), BF),
            v((NY, 32, 128), F32),
            v((3, NY, 2 * TOK, WIDE), BF),
            v((3, NQ, two, WIDE), BF),
            v((3, NQ, two, WIDE), BF),
            v((2, NQ, two, WIDE), BF),
            v((2, NQ, two, WIDE), BF),
            v((two * NQ, HID), F32),
            v((two * NQ, HID), BF),
            v((SLOT * NQ, HID), F32),
            v((SLOT * NQ, D), BF),
            v((SLOT * NQ, HID), BF),
            v((2, SLOT * NQ, NY * TOK), BF),
            v((SLOT * NQ, 128), F32),
            v((2, 2, NY * TOK, two * NQ), BF),
            v((2, NY, 2 * TOK, WIDE), F32),
            v((2, 4, 2, 2 * TOK, WIDE), BF),
            v((2, 4, 2, 2 * TOK, WIDE), BF),
            v((2, TOK, D), BF),
            v((2, TOK, D), BF),
            v((PIECES, WIDE // PIECES, HID), BF),
            v((PIECES, WIDE // PIECES, HID), BF),
            dma,
            dma((NY,)), dma((NY,)),
            dma((3, 4, 2)), dma((3, 4, 2)),
            dma((3, NQ)), dma((3, NQ)),
            dma((2, NQ)), dma((2, NQ)),
            dma((2, 4, 2)), dma((2, 4, 2)),
            dma((PIECES,)), dma((PIECES,)),
            dma((2,)), dma((2,)),
        ],
        compiler_params=pltpu.CompilerParams(
            collective_id=0, has_side_effects=True, vmem_limit_bytes=58 << 20
        ),
        cost_estimate=pl.CostEstimate(flops=8 * 10**9, bytes_accessed=10**7, transcendentals=10**6),
        name="relay",
    )(meta, s, o, f, w)


def on_device(section_inputs, saved_inputs, output_grads, forward_routes, backward_routes,
              forward_gates, backward_gates, expert_weights):
    rows = jnp.concatenate(
        [forward_routes[0].astype(F32), backward_routes[0].astype(F32), forward_gates[0], backward_gates[0]], axis=1
    ).T
    meta = jnp.concatenate([rows] * 4, axis=1)
    after, prior, wg = relay(meta, saved_inputs[0], output_grads[0], section_inputs[0], expert_weights[0, 0])
    return after[None], prior[None], wg[None, None]


def solution(mesh):
    placed = P("pipe", ("expert", "dp"), None)
    return jax.shard_map(
        on_device,
        mesh=mesh,
        in_specs=(placed,) * 7 + (P("pipe", "expert", None, None),),
        out_specs=(placed, placed, P("pipe", "expert", "dp", None)),
        check_vma=False,
    )
```

```python
import functools

import jax
import jax.numpy as jnp
from jax import lax
from jax.experimental import pallas as pl
from jax.experimental.pallas import tpu as pltpu
from jax.sharding import PartitionSpec as P

MESH = pl.DeviceIdType.MESH
BF = jnp.bfloat16
F32 = jnp.float32
TOK = 32
CAP = 5
NY = 8
NQ = 8
WIDE = 1024
PAIRS = ((1, 7), (2, 6), (3, 5))
SLOT = NY * CAP
D = 2048
HID = 768
PIECES = 8
ORDER = (4, 5, 2, 3, 6, 7, 1)


def dot(a, b):
    return jnp.dot(a, b, preferred_element_type=F32)


def dot_t(a, b):
    return lax.dot_general(a, b, (((1,), (1,)), ((), ())), preferred_element_type=F32)


def dot_tl(a, b):
    return lax.dot_general(a, b, (((0,), (0,)), ((), ())), preferred_element_type=F32)


def tile(i, n):
    return pl.ds(pl.multiple_of(i * n, n), n)


def div(v, n):
    return lax.shift_right_logical(v * (-(-65536 // n)), 16)


def iota(shape, axis):
    return lax.broadcasted_iota(jnp.int32, shape, axis)


def kernel(
    rf_ref, rb_ref, gf_ref, gb_ref, s_hbm, o_hbm, f_hbm, w_hbm,
    next_ref, prior_ref, wg_ref,
    w, metas, xsg, xf, gsend, grecv, osend, orecv, first, fsend, frecv, rsend, rrecv, rows, pair, frow, fh,
    big, scale, undo, undo1, pack, comb, part, ysend, yrecv, out_send, out_recv, wsend, wrecv, wown,
    w_sem, in_sem, out_sem, ms, mr, gs, gr, xs, xr, bs, br, ys, yr, ds_, dr, ps, pr,
):
    e = lax.axis_index("expert")
    p = lax.axis_index("pipe")
    half = lax.axis_index("dp")
    y, q = e // NQ, e % NQ
    x, c = q // 2, q % 2

    def ydev(k):
        return {"expert": ((y + k + NY) % NY) * NQ + q}

    def qdev(j):
        jx, jc = j // 2, j % 2
        other = ((x // 2 + jx // 2) % 2) * 2 + (x % 2 + jx % 2) % 2
        return {"expert": y * NQ + other * 2 + (c + jc) % 2}

    def send(src, dst, ssem, rsem, dev):
        return pltpu.make_async_remote_copy(
            src_ref=src, dst_ref=dst, send_sem=ssem, recv_sem=rsem, device_id=dev, device_id_type=MESH
        )

    sent = []

    def start(copy):
        copy.start()
        sent.append(copy)
        return copy

    def arrive(copies):
        for copy in copies:
            copy.wait_recv()

    barrier = pltpu.get_barrier_semaphore()
    friends = [ydev(k) for k in range(1, NY)] + [qdev(j) for j in range(1, NQ)]
    friends += [{"dp": 1 - half}, {"pipe": (p + 1) % 4}, {"pipe": (p + 3) % 4}]
    for dev in friends:
        pl.semaphore_signal(barrier, inc=1, device_id=dev, device_id_type=MESH)

    inputs = [
        pltpu.make_async_copy(u, v, in_sem.at[i])
        for i, (u, v) in enumerate((
            (s_hbm, xsg.at[0, pl.ds(0, TOK)]),
            (o_hbm, xsg.at[0, pl.ds(TOK, TOK)]),
            (f_hbm.at[:, pl.ds(0, WIDE)], xf.at[0, pl.ds(0, TOK)]),
            (f_hbm.at[:, pl.ds(WIDE, WIDE)], xf.at[0, pl.ds(TOK, TOK)]),
        ))
    ]
    for copy in inputs:
        copy.start()
    w_copy = pltpu.make_async_copy(w_hbm, w, w_sem)
    w_copy.start()

    metas[0] = jnp.concatenate(
        [rf_ref[...].astype(F32), rb_ref[...].astype(F32), gf_ref[...], gb_ref[...]], axis=1
    )

    lane = div(iota((8, 128), 1), TOK)

    def lanes_of(kind, blocks):
        v = None
        for b, d in enumerate(blocks):
            shift = ((b - kind) * TOK) % 128
            u = metas[d]
            if shift:
                u = pltpu.roll(u, shift, 1)
            v = u if v is None else jnp.where(lane == b, u, v)
        return v

    expert = (y * NQ + jnp.bitwise_xor(iota((NQ, 128), 0), q)).astype(F32)

    def routed(t, blocks):
        routes, gates = lanes_of(t, blocks), lanes_of(2 + t, blocks)
        mark = jnp.zeros((NQ, 128), F32)
        gate = jnp.zeros((NQ, 128), F32)
        for k in range(8):
            same = routes[k : k + 1, :] == expert
            mark = mark + jnp.where(same, 1.0, 0.0)
            gate = gate + jnp.where(same, gates[k : k + 1, :], 0.0)
        return mark, gate

    r2, l2 = iota((128, 128), 0), iota((128, 128), 1)
    earlier = jnp.where((div(r2, TOK) == div(l2, TOK)) & (r2 < l2), 1.0, 0.0).astype(BF)

    def places_of(marks):
        return jnp.where(marks > 0.5, dot(marks.astype(BF), earlier), -1.0)

    spread = jnp.where(iota((640, NQ), 1) == div(iota((640, NQ), 0), 80), 1.0, 0.0)

    def prepare(n, spot, gate):
        r, l = iota((640, 128), 0), iota((640, 128), 1)
        r = r - div(r, 80) * 80
        l64 = div(l, 64)
        single = n in (0, 4)
        count = 10 if single else 20
        part_of = div(r, count)
        r = r - part_of * count
        tensor = div(r, count // 2)
        r = r - tensor * (count // 2)
        fits = div(l, TOK) - 2 * l64 == tensor
        if not single:
            b2 = div(r, CAP)
            fits = fits & (l64 == b2)
            r = r - b2 * CAP
        want = jnp.where(fits, r, -2).astype(F32)
        where = dot(spread.astype(BF), spot.astype(BF))
        hit = jnp.where(where == want, 1.0, 0.0)
        gate = jnp.dot(spread, gate, preferred_element_type=F32, precision=lax.Precision.HIGHEST)
        counted = jnp.where(l64 == 0, hit * gate, 0.0) if single else hit * gate
        total = jnp.sum(counted, axis=1, keepdims=True)
        scale[n] = jnp.where(tensor == 0, 1.0, jnp.broadcast_to(total, (640, 128)))
        for i in range(4):
            here = part_of == (2 * i + l64 if single else i)
            big[n, :, i * 128 : (i + 1) * 128] = jnp.where(here, hit, 0.0).astype(BF)

    def pack_single(n, d, k):
        stack = [xsg[d, :, i * 256 : (i + 1) * 256] for i in range(8)]
        v = dot(big[n], jnp.concatenate(stack, axis=0)) * scale[n, :, 0:1]
        v = v.astype(BF).reshape(NQ, 80, 256)
        orecv[k, 0] = v[0]
        osend[k, 1:] = v[1:]

    def send_single(n, k):
        return [start(send(osend.at[k, j], orecv.at[k, j], xs.at[n, j], xr.at[n, j], qdev(j))) for j in ORDER]

    mark, gate = routed(1, (0, 0, 0, 0))
    prepare(0, places_of(mark), gate)
    inputs[0].wait()
    inputs[1].wait()
    pack_single(0, 0, 0)

    pl.semaphore_wait(barrier, len(friends))

    def gather(i, step):
        buf = (xsg, xf)[i]
        copies = []
        for way in range(2):
            src, dst = ((NY - step + 1) % NY, NY - step) if way == 0 else (step - 1, step)
            if step < 4:
                a, b = buf.at[src], buf.at[dst]
            else:
                cut = pl.ds(way * TOK, TOK)
                a, b = buf.at[src, cut], buf.at[dst, cut]
            copies.append(start(send(a, b, gs.at[i, step - 1, way], gr.at[i, step - 1, way], ydev(1 - 2 * way))))
        return copies

    for k in (1, 7, 2, 6, 3, 5, 4):
        start(send(metas.at[0], metas.at[NY - k], ms.at[k], mr.at[NY - k], ydev(k)))
    g = {0: gather(0, 1)}

    gx = {0: send_single(0, 0)}
    inputs[2].wait()
    inputs[3].wait()

    def order(width):
        m, a = iota((640, 640), 1), iota((640, 640), 0)
        i = div(a, 8 * width)
        a = a - i * 8 * width
        tensor = div(a, 4 * width)
        a = a - tensor * 4 * width
        j = div(a, width // 2)
        a = a - j * (width // 2)
        return jnp.where(m == j * 80 + i * width + tensor * (width // 2) + a, 1.0, 0.0).astype(BF)

    undo[...] = order(20)

    for k in range(1, NY):
        send(metas.at[0], metas.at[k], ms.at[k], mr.at[k], ydev(k)).wait_recv()

    sets = [(1, (u, u, v, v)) for u, v in PAIRS] + [(1, (4, 4, 4, 4))]
    sets += [(t, tuple(range(4 * h, 4 * h + 4))) for t in range(2) for h in range(2)]
    found = [routed(*one) for one in sets]
    place = places_of(jnp.concatenate([one[0] for one in found], axis=0))
    places = [place[n * NQ : (n + 1) * NQ] for n in range(8)]
    gated = [one[1] for one in found]

    def dispatch(n):
        @pl.loop(0, 2)
        def _(h):
            stack = [
                xsg[d, :, pl.ds(pl.multiple_of(i * 512 + h * 256, 256), 256)]
                for i in range(4) for d in PAIRS[n - 1]
            ]
            v = dot(big[n], jnp.concatenate(stack, axis=0)) * scale[n, :, 0:1]
            v = v.astype(BF).reshape(NQ, 80, 256)
            grecv[n - 1, 0, :, tile(h, 256)] = v[0]
            gsend[n - 1, 1:, :, tile(h, 256)] = v[1:]

        return [
            start(send(gsend.at[n - 1, j], grecv.at[n - 1, j], xs.at[n, j], xr.at[n, j], qdev(j))) for j in ORDER
        ]

    def forward(step):
        arrive(g[1])
        g[1] = gather(1, step)

    wide = NY * TOK

    def full(v, t):
        return jnp.concatenate([v[4 + 2 * t], v[5 + 2 * t]], axis=1)

    zeros = jnp.zeros((SLOT, wide), F32)

    def slots(t):
        rr, ll = iota((SLOT, wide), 0), iota((SLOT, wide), 1)
        block = div(rr, CAP)
        d = block
        if t == 1:
            up = div(block, 2)
            d = jnp.where(block == 2 * up, up + 1, NY - 1 - up)
            d = jnp.where(block == 6, 0, jnp.where(block == 7, 4, d))
        target = jnp.where(div(ll, TOK) == d, rr - block * CAP, -2).astype(F32)
        ones, lefts, rights = [], [], []
        spot, gate = full(places, t), full(gated, t)
        for j in range(NQ):
            hit = jnp.where(spot[j : j + 1, :] == target, 1.0, 0.0)
            weight = hit * gate[j : j + 1, :] if t == 0 else hit
            ones.append(hit)
            lefts += [weight, zeros]
            rights += [zeros, weight]
        if t == 0:
            pack[...] = jnp.concatenate(ones, axis=0).astype(BF)
        comb[t, 0] = jnp.concatenate(lefts, axis=0).T.astype(BF)
        comb[t, 1] = jnp.concatenate(rights, axis=0).T.astype(BF)

    def hidden(n):
        @pl.loop(0, HID // 256)
        def _(k):
            v = dot(rows[n], w[:, tile(k, 256)])
            h, a = v[0:80], v[80:160]
            s = jax.nn.sigmoid(h)
            hg = a * s * (1.0 + h * (1.0 - s))
            pair[n, :, tile(k, 256)] = jnp.concatenate([hg, h * s], axis=0).astype(BF)

    def receive(n):
        arrive(gx[n])

        @pl.loop(0, 2)
        def _(h):
            v = dot(undo[...], grecv[n - 1, :, :, tile(h, 256)].reshape(640, 256)).astype(BF)
            for i in range(4):
                rows[n - 1, :, pl.ds(pl.multiple_of(i * 512 + h * 256, 256), 256)] = v[i * 160 : (i + 1) * 160]

        hidden(n - 1)

    for n in range(1, 5):
        prepare(n, places[n - 1], gated[n - 1])
        arrive(g[0])
        if n < 4:
            g[0] = gather(0, n + 1)
            if n == 3:
                g[1] = gather(1, 1)
            gx[n] = dispatch(n)
        else:
            pack_single(4, 4, 1)
            gx[4] = send_single(4, 1)
            forward(2)
        if n == 1:
            slots(0)
            undo1[...] = order(10)
            slots(1)
            w_copy.wait()
        elif n == 2:
            arrive(gx[0])
            first[...] = dot(undo1[...], orecv[0].reshape(640, 256))
            receive(1)
        else:
            receive(n - 1)

    forward(3)
    arrive(gx[4])
    last = dot(undo1[...], orecv[1].reshape(640, 256))
    for i in range(8):
        pieces = [v[i * 80 + h : i * 80 + h + 40] for h in (0, 40) for v in (first, last)]
        rows[3, :, i * 256 : (i + 1) * 256] = jnp.concatenate(pieces, axis=0).astype(BF)
    forward(4)
    hidden(3)

    per = WIDE // PIECES

    def weight_part(owner, k):
        at = pl.ds(pl.multiple_of(owner * WIDE + k * per, per), per)
        return dot_tl(rows[:, :, at].reshape(640, per), pair[...].reshape(640, HID)).astype(BF)

    wcopies = []

    def other_half(k):
        wsend[k] = weight_part(1 - half, k)
        wcopies.append(start(send(wsend.at[k], wrecv.at[k], ds_.at[k], dr.at[k], {"dp": 1 - half})))

    other_half(0)
    other_half(1)
    arrive(g[1])

    @pl.loop(0, WIDE // 256)
    def _(n):
        at = tile(n, 256)
        top = dot(pack[...], xf[:, 0:TOK, at].reshape(wide, 256))
        low = dot(pack[...], xf[:, TOK : 2 * TOK, at].reshape(wide, 256))
        for j in range(NQ):
            cut = slice(j * SLOT, (j + 1) * SLOT)
            msg = jnp.concatenate([top[cut], low[cut]], axis=0).astype(BF)
            if j == 0:
                frecv[0, :, at] = msg
            else:
                fsend[j, :, at] = msg

    fx = [start(send(fsend.at[j], frecv.at[j], xs.at[5, j], xr.at[5, j], qdev(j))) for j in ORDER]

    def give_back(t, source):
        copies = []
        for h in range(2):
            unit = 2 * t + h

            @pl.loop(0, 2)
            def _(n):
                at = tile(n, 256)
                left = dot_t(source, w[pl.ds(pl.multiple_of(h * 512 + n * 256, 256), 256), :])
                right = dot_t(source, w[pl.ds(pl.multiple_of(WIDE + h * 512 + n * 256, 256), 256), :])
                for j in range(NQ):
                    cut = slice(j * SLOT, (j + 1) * SLOT)
                    msg = jnp.concatenate([left[cut], right[cut]], axis=0).astype(BF)
                    if j == 0:
                        rrecv[unit, 0, :, at] = msg
                    else:
                        rsend[unit, j, :, at] = msg

            copies.append([
                start(send(rsend.at[unit, j], rrecv.at[unit, j], bs.at[unit, j], br.at[unit, j], qdev(j)))
                for j in ORDER
            ])
        return copies

    a = iota((320, 320), 0)
    j8 = div(a, 40)
    a = a - j8 * 40
    n4 = div(a, 10)
    a = a - n4 * 10
    b2 = div(a, CAP)
    source = jnp.where(n4 < 3, n4 * 80 + j8 * 10 + a, 240 + b2 * 40 + j8 * CAP + (a - b2 * CAP))
    turn = jnp.where(iota((320, 320), 1) == source, 1.0, 0.0).astype(BF)
    b1 = give_back(1, dot(turn, pair[:, 0:80, :].reshape(320, HID)).astype(BF))

    for k in range(2, PIECES):
        other_half(k)

    arrive(fx)

    @pl.loop(0, WIDE // 256)
    def _(n):
        v = frecv[:, :, tile(n, 256)].astype(F32)
        frow[:, tile(n, 256)] = v[:, 0:SLOT].reshape(SLOT * NQ, 256).astype(BF)
        frow[:, pl.ds(pl.multiple_of(WIDE + n * 256, 256), 256)] = v[:, SLOT:].reshape(SLOT * NQ, 256).astype(BF)

    @pl.loop(0, HID // 256)
    def _(n):
        h = dot(frow[...], w[:, tile(n, 256)])
        fh[:, tile(n, 256)] = (h * jax.nn.sigmoid(h)).astype(BF)

    b0 = give_back(0, fh[...])

    def combine(u):
        @pl.loop(0, 2)
        def _(n):
            at = tile(n, 256)
            got = rrecv[u, :, :, at].reshape(2 * SLOT * NQ, 256)
            part[u, :, 0:TOK, at] = dot(comb[u // 2, 0], got).reshape(NY, TOK, 256)
            part[u, :, TOK : 2 * TOK, at] = dot(comb[u // 2, 1], got).reshape(NY, TOK, 256)

    r = {}

    def reduce_step(u, step):
        copies = []
        for way in range(2):
            if step == 1:
                cut = slice(way * TOK, (way + 1) * TOK)
                ysend[u, 0, way, cut] = part[u, 4, cut].astype(BF)
                where = pl.ds(way * TOK, TOK)
                a, b = ysend.at[u, 0, way, where], yrecv.at[u, 0, way, where]
            else:
                s = step - 1
                r[u][way].wait_recv()
                d = 5 - step if way == 0 else 3 + step
                if step == 2:
                    got = slice(way * TOK, (way + 1) * TOK)
                    rest = slice((1 - way) * TOK, (2 - way) * TOK)
                    ysend[u, s, way, got] = (part[u, d, got] + yrecv[u, 0, way, got].astype(F32)).astype(BF)
                    ysend[u, s, way, rest] = part[u, d, rest].astype(BF)
                else:
                    ysend[u, s, way] = (part[u, d] + yrecv[u, s - 1, way].astype(F32)).astype(BF)
                a, b = ysend.at[u, s, way], yrecv.at[u, s, way]
            copies.append(start(send(a, b, ys.at[u, step - 1, way], yr.at[u, step - 1, way], ydev(1 - 2 * way))))
        r[u] = copies

    pipes = {}

    def finish(u):
        arrive(r[u])
        total = part[u, 0] + yrecv[u, 3, 0].astype(F32) + yrecv[u, 3, 1].astype(F32)
        t, h = u // 2, u % 2
        for i in range(2):
            if t == 1:
                base = xsg[0, TOK : 2 * TOK, i * WIDE + h * 512 : i * WIDE + h * 512 + 512]
            else:
                base = xf[0, i * TOK : (i + 1) * TOK, h * 512 : h * 512 + 512]
            cut = slice(i * TOK, (i + 1) * TOK)
            out_send[u, cut] = (base.astype(F32) + total[cut]).astype(BF)
        to = (p + (3 if t == 1 else 1)) % 4
        pipes[u] = start(send(out_send.at[u], out_recv.at[u], ps.at[u], pr.at[u], {"pipe": to}))

    def own_half(k):
        wown[k] = weight_part(half, k)

    outs = []

    def place_out(src, dst):
        copy = pltpu.make_async_copy(src, dst, out_sem.at[len(outs)])
        copy.start()
        outs.append(copy)

    def sum_half(k):
        wcopies[k].wait_recv()
        wown[k] = (wown[k].astype(F32) + wrecv[k].astype(F32)).astype(BF)
        place_out(wown.at[k], wg_ref.at[pl.ds(k * per, per)])

    waits = {2: b1[0], 3: b1[1], 0: b0[0], 1: b0[1]}
    begun = {2: 0, 3: 2, 0: 4, 1: 6}
    pieces = list(range(PIECES))
    for tick in range(11):
        for u in (2, 3, 0, 1):
            step = tick - begun[u] + 1
            if step == 1:
                arrive(waits[u])
                combine(u)
            if 1 <= step <= 4:
                reduce_step(u, step)
            if step == 5:
                finish(u)
        for _ in range(2):
            if pieces:
                own_half(pieces.pop(0))
        if tick in (4, 6, 8, 9):
            sum_half((4, 6, 8, 9).index(tick))

    def take(u):
        pipes[u].wait_recv()
        out = prior_ref if u >= 2 else next_ref
        for i in range(2):
            place_out(out_recv.at[u, pl.ds(i * TOK, TOK)], out.at[:, pl.ds(i * WIDE + (u % 2) * 512, 512)])

    take(2)
    take(3)
    for k in range(4, PIECES):
        sum_half(k)
    take(0)
    take(1)
    for copy in outs:
        copy.wait()
    for copy in sent:
        copy.wait_send()


def finish_kernel(a, b, c, x, y, z, va, vb, vc, sems):
    pieces = [(c.at[pl.ds(i * 256, 256)], vc.at[i], z.at[pl.ds(i * 256, 256)]) for i in range(4)]
    pieces += [(a, va, x), (b, vb, y)]
    loads = [pltpu.make_async_copy(u, m, sems.at[0, i]) for i, (u, m, _) in enumerate(pieces)]
    stores = [pltpu.make_async_copy(m, o, sems.at[1, i]) for i, (_, m, o) in enumerate(pieces)]
    for copy in loads:
        copy.start()
    for load, store in zip(loads, stores):
        load.wait()
        store.start()
    for copy in stores:
        copy.wait()


def relay(rf, rb, gf, gb, s, o, f, w):
    vmem = pl.BlockSpec(memory_space=pltpu.VMEM)
    dma = pltpu.SemaphoreType.DMA
    v = pltpu.VMEM
    two = 2 * SLOT
    return pl.pallas_call(
        kernel,
        out_shape=(
            jax.ShapeDtypeStruct((TOK, D), BF),
            jax.ShapeDtypeStruct((TOK, D), BF),
            jax.ShapeDtypeStruct((D // 2, HID), BF),
        ),
        in_specs=[vmem] * 4 + [pl.BlockSpec(memory_space=pl.ANY)] * 4,
        out_specs=(pl.BlockSpec(memory_space=pl.ANY),) * 3,
        scratch_shapes=[
            v((D, HID), BF),
            v((NY, 8, 128), F32),
            v((NY, 2 * TOK, D), BF),
            v((NY, 2 * TOK, WIDE), BF),
            v((3, NQ, two, 512), BF),
            v((3, NQ, two, 512), BF),
            v((2, NQ, two, 256), BF),
            v((2, NQ, two, 256), BF),
            v((640, 256), F32),
            v((NQ, two, WIDE), BF),
            v((NQ, two, WIDE), BF),
            v((4, NQ, two, 512), BF),
            v((4, NQ, two, 512), BF),
            v((4, 160, D), BF),
            v((4, 160, HID), BF),
            v((SLOT * NQ, D), BF),
            v((SLOT * NQ, HID), BF),
            v((5, 640, 512), BF),
            v((5, 640, 128), F32),
            v((640, 640), BF),
            v((640, 640), BF),
            v((SLOT * NQ, NY * TOK), BF),
            v((2, 2, NY * TOK, two * NQ), BF),
            v((4, NY, 2 * TOK, 512), F32),
            v((4, 4, 2, 2 * TOK, 512), BF),
            v((4, 4, 2, 2 * TOK, 512), BF),
            v((4, 2 * TOK, 512), BF),
            v((4, 2 * TOK, 512), BF),
            v((PIECES, WIDE // PIECES, HID), BF),
            v((PIECES, WIDE // PIECES, HID), BF),
            v((PIECES, WIDE // PIECES, HID), BF),
            dma,
            dma((4,)),
            dma((PIECES + 8,)),
            dma((NY,)), dma((NY,)),
            dma((2, 4, 2)), dma((2, 4, 2)),
            dma((6, NQ)), dma((6, NQ)),
            dma((4, NQ)), dma((4, NQ)),
            dma((4, 4, 2)), dma((4, 4, 2)),
            dma((PIECES,)), dma((PIECES,)),
            dma((4,)), dma((4,)),
        ],
        compiler_params=pltpu.CompilerParams(
            collective_id=0, has_side_effects=True, vmem_limit_bytes=58 << 20
        ),
        cost_estimate=pl.CostEstimate(flops=8 * 10**9, bytes_accessed=10**7, transcendentals=10**6),
        name="relay",
    )(rf, rb, gf, gb, s, o, f, w)


def on_device(section_inputs, saved_inputs, output_grads, forward_routes, backward_routes,
              forward_gates, backward_gates, expert_weights):
    outs = relay(
        forward_routes[0].T, backward_routes[0].T, forward_gates[0].T, backward_gates[0].T,
        saved_inputs[0], output_grads[0], section_inputs[0], expert_weights[0, 0],
    )
    anywhere = pl.BlockSpec(memory_space=pl.ANY)
    after, prior, wg = pl.pallas_call(
        finish_kernel,
        out_shape=[jax.ShapeDtypeStruct(v.shape, v.dtype) for v in outs],
        in_specs=[anywhere] * 3,
        out_specs=[anywhere] * 3,
        scratch_shapes=[
            pltpu.VMEM((TOK, D), BF),
            pltpu.VMEM((TOK, D), BF),
            pltpu.VMEM((4, 256, HID), BF),
            pltpu.SemaphoreType.DMA((2, 6)),
        ],
        name="place",
    )(*outs)
    return after[None], prior[None], wg[None, None]


def solution(mesh):
    placed = P("pipe", ("expert", "dp"), None)
    return jax.shard_map(
        on_device,
        mesh=mesh,
        in_specs=(placed,) * 7 + (P("pipe", "expert", None, None),),
        out_specs=(placed, placed, P("pipe", "expert", "dp", None)),
        check_vma=False,
    )
```

```python
import functools

import jax
import jax.numpy as jnp
from jax import lax
from jax.experimental import pallas as pl
from jax.experimental.pallas import tpu as pltpu
from jax.sharding import PartitionSpec as P

MESH = pl.DeviceIdType.MESH
BF = jnp.bfloat16
F32 = jnp.float32
TOK = 32
CAP = 5
NY = 8
NQ = 8
WIDE = 1024
PAIRS = ((1, 7), (2, 6), (3, 5))
SLOT = NY * CAP
D = 2048
HID = 768
PIECES = 8
ORDER = (4, 5, 2, 3, 6, 7, 1)


def dot(a, b):
    return jnp.dot(a, b, preferred_element_type=F32)


def dot_t(a, b):
    return lax.dot_general(a, b, (((1,), (1,)), ((), ())), preferred_element_type=F32)


def dot_tl(a, b):
    return lax.dot_general(a, b, (((0,), (0,)), ((), ())), preferred_element_type=F32)


def tile(i, n):
    return pl.ds(pl.multiple_of(i * n, n), n)


def div(v, n):
    return lax.shift_right_logical(v * (-(-65536 // n)), 16)


def iota(shape, axis):
    return lax.broadcasted_iota(jnp.int32, shape, axis)


def kernel(
    rf_ref, rb_ref, gf_ref, gb_ref, s_hbm, o_hbm, f_hbm, w_hbm,
    next_ref, prior_ref, wg_ref,
    w, metas, xsg, xf, gsend, grecv, osend, orecv, first, fsend, frecv, rsend, rrecv, rows, pair, frow, fh,
    big, scale, undo, undo1, pack, comb, part, ysend, yrecv, out_send, out_recv, wsend, wrecv, wown,
    w_sem, in_sem, out_sem, ms, mr, gs, gr, xs, xr, bs, br, ys, yr, ds_, dr, ps, pr,
):
    e = lax.axis_index("expert")
    p = lax.axis_index("pipe")
    half = lax.axis_index("dp")
    y, q = e // NQ, e % NQ
    x, c = q // 2, q % 2

    def ydev(k):
        return {"expert": ((y + k + NY) % NY) * NQ + q}

    def qdev(j):
        jx, jc = j // 2, j % 2
        other = ((x // 2 + jx // 2) % 2) * 2 + (x % 2 + jx % 2) % 2
        return {"expert": y * NQ + other * 2 + (c + jc) % 2}

    def send(src, dst, ssem, rsem, dev):
        return pltpu.make_async_remote_copy(
            src_ref=src, dst_ref=dst, send_sem=ssem, recv_sem=rsem, device_id=dev, device_id_type=MESH
        )

    sent = []

    def start(copy):
        copy.start()
        sent.append(copy)
        return copy

    def arrive(copies):
        for copy in copies:
            copy.wait_recv()

    barrier = pltpu.get_barrier_semaphore()
    friends = [ydev(k) for k in range(1, NY)] + [qdev(j) for j in range(1, NQ)]
    friends += [{"dp": 1 - half}, {"pipe": (p + 1) % 4}, {"pipe": (p + 3) % 4}]
    for dev in friends:
        pl.semaphore_signal(barrier, inc=1, device_id=dev, device_id_type=MESH)

    inputs = [
        pltpu.make_async_copy(u, v, in_sem.at[i])
        for i, (u, v) in enumerate((
            (s_hbm, xsg.at[0, pl.ds(0, TOK)]),
            (o_hbm, xsg.at[0, pl.ds(TOK, TOK)]),
            (f_hbm.at[:, pl.ds(0, WIDE)], xf.at[0, pl.ds(0, TOK)]),
            (f_hbm.at[:, pl.ds(WIDE, WIDE)], xf.at[0, pl.ds(TOK, TOK)]),
        ))
    ]
    for copy in inputs:
        copy.start()
    w_copy = pltpu.make_async_copy(w_hbm, w, w_sem)
    w_copy.start()

    metas[0] = jnp.concatenate(
        [rf_ref[...].astype(F32), rb_ref[...].astype(F32), gf_ref[...], gb_ref[...]], axis=1
    )

    lane = div(iota((8, 128), 1), TOK)

    def lanes_of(kind, blocks):
        v = None
        for b, d in enumerate(blocks):
            shift = ((b - kind) * TOK) % 128
            u = metas[d]
            if shift:
                u = pltpu.roll(u, shift, 1)
            v = u if v is None else jnp.where(lane == b, u, v)
        return v

    expert = (y * NQ + jnp.bitwise_xor(iota((NQ, 128), 0), q)).astype(F32)

    def routed(t, blocks):
        routes, gates = lanes_of(t, blocks), lanes_of(2 + t, blocks)
        mark = jnp.zeros((NQ, 128), F32)
        gate = jnp.zeros((NQ, 128), F32)
        for k in range(8):
            same = routes[k : k + 1, :] == expert
            mark = mark + jnp.where(same, 1.0, 0.0)
            gate = gate + jnp.where(same, gates[k : k + 1, :], 0.0)
        return mark, gate

    r2, l2 = iota((128, 128), 0), iota((128, 128), 1)
    earlier = jnp.where((div(r2, TOK) == div(l2, TOK)) & (r2 < l2), 1.0, 0.0).astype(BF)

    def places_of(marks):
        return jnp.where(marks > 0.5, dot(marks.astype(BF), earlier), -1.0)

    spread = jnp.where(iota((640, NQ), 1) == div(iota((640, NQ), 0), 80), 1.0, 0.0)

    def prepare(n, spot, gate):
        r, l = iota((640, 128), 0), iota((640, 128), 1)
        r = r - div(r, 80) * 80
        l64 = div(l, 64)
        single = n in (0, 4)
        count = 10 if single else 20
        part_of = div(r, count)
        r = r - part_of * count
        tensor = div(r, count // 2)
        r = r - tensor * (count // 2)
        fits = div(l, TOK) - 2 * l64 == tensor
        if not single:
            b2 = div(r, CAP)
            fits = fits & (l64 == b2)
            r = r - b2 * CAP
        want = jnp.where(fits, r, -2).astype(F32)
        where = dot(spread.astype(BF), spot.astype(BF))
        hit = jnp.where(where == want, 1.0, 0.0)
        gate = jnp.dot(spread, gate, preferred_element_type=F32, precision=lax.Precision.HIGHEST)
        counted = jnp.where(l64 == 0, hit * gate, 0.0) if single else hit * gate
        total = jnp.sum(counted, axis=1, keepdims=True)
        scale[n] = jnp.where(tensor == 0, 1.0, jnp.broadcast_to(total, (640, 128)))
        for i in range(4):
            here = part_of == (2 * i + l64 if single else i)
            big[n, :, i * 128 : (i + 1) * 128] = jnp.where(here, hit, 0.0).astype(BF)

    def pack_single(n, d, k):
        stack = [xsg[d, :, i * 256 : (i + 1) * 256] for i in range(8)]
        v = dot(big[n], jnp.concatenate(stack, axis=0)) * scale[n, :, 0:1]
        v = v.astype(BF).reshape(NQ, 80, 256)
        orecv[k, 0] = v[0]
        osend[k, 1:] = v[1:]

    def send_single(n, k):
        return [start(send(osend.at[k, j], orecv.at[k, j], xs.at[n, j], xr.at[n, j], qdev(j))) for j in ORDER]

    mark, gate = routed(1, (0, 0, 0, 0))
    prepare(0, places_of(mark), gate)
    inputs[0].wait()
    inputs[1].wait()
    pack_single(0, 0, 0)

    pl.semaphore_wait(barrier, len(friends))

    def gather(i, step):
        buf = (xsg, xf)[i]
        copies = []
        for way in range(2):
            src, dst = ((NY - step + 1) % NY, NY - step) if way == 0 else (step - 1, step)
            if step < 4:
                a, b = buf.at[src], buf.at[dst]
            else:
                cut = pl.ds(way * TOK, TOK)
                a, b = buf.at[src, cut], buf.at[dst, cut]
            copies.append(start(send(a, b, gs.at[i, step - 1, way], gr.at[i, step - 1, way], ydev(1 - 2 * way))))
        return copies

    for k in (1, 7, 2, 6, 3, 5, 4):
        start(send(metas.at[0], metas.at[NY - k], ms.at[k], mr.at[NY - k], ydev(k)))
    g = {0: gather(0, 1)}

    gx = {0: send_single(0, 0)}
    inputs[2].wait()
    inputs[3].wait()
    g[1] = gather(1, 1)

    def order(width):
        m, a = iota((640, 640), 1), iota((640, 640), 0)
        i = div(a, 8 * width)
        a = a - i * 8 * width
        tensor = div(a, 4 * width)
        a = a - tensor * 4 * width
        j = div(a, width // 2)
        a = a - j * (width // 2)
        return jnp.where(m == j * 80 + i * width + tensor * (width // 2) + a, 1.0, 0.0).astype(BF)

    undo[...] = order(20)

    for k in range(1, NY):
        send(metas.at[0], metas.at[k], ms.at[k], mr.at[k], ydev(k)).wait_recv()

    sets = [(1, (u, u, v, v)) for u, v in PAIRS] + [(1, (4, 4, 4, 4))]
    sets += [(t, tuple(range(4 * h, 4 * h + 4))) for t in range(2) for h in range(2)]
    found = [routed(*one) for one in sets]
    place = places_of(jnp.concatenate([one[0] for one in found], axis=0))
    places = [place[n * NQ : (n + 1) * NQ] for n in range(8)]
    gated = [one[1] for one in found]

    def dispatch(n):
        @pl.loop(0, 2)
        def _(h):
            stack = [
                xsg[d, :, pl.ds(pl.multiple_of(i * 512 + h * 256, 256), 256)]
                for i in range(4) for d in PAIRS[n - 1]
            ]
            v = dot(big[n], jnp.concatenate(stack, axis=0)) * scale[n, :, 0:1]
            v = v.astype(BF).reshape(NQ, 80, 256)
            grecv[n - 1, 0, :, tile(h, 256)] = v[0]
            gsend[n - 1, 1:, :, tile(h, 256)] = v[1:]

        return [
            start(send(gsend.at[n - 1, j], grecv.at[n - 1, j], xs.at[n, j], xr.at[n, j], qdev(j))) for j in ORDER
        ]

    def forward(step):
        arrive(g[1])
        g[1] = gather(1, step)

    wide = NY * TOK

    def full(v, t):
        return jnp.concatenate([v[4 + 2 * t], v[5 + 2 * t]], axis=1)

    zeros = jnp.zeros((SLOT, wide), F32)

    def slots(t):
        rr, ll = iota((SLOT, wide), 0), iota((SLOT, wide), 1)
        block = div(rr, CAP)
        d = block
        if t == 1:
            up = div(block, 2)
            d = jnp.where(block == 2 * up, up + 1, NY - 1 - up)
            d = jnp.where(block == 6, 0, jnp.where(block == 7, 4, d))
        target = jnp.where(div(ll, TOK) == d, rr - block * CAP, -2).astype(F32)
        ones, lefts, rights = [], [], []
        spot, gate = full(places, t), full(gated, t)
        for j in range(NQ):
            hit = jnp.where(spot[j : j + 1, :] == target, 1.0, 0.0)
            weight = hit * gate[j : j + 1, :] if t == 0 else hit
            ones.append(hit)
            lefts += [weight, zeros]
            rights += [zeros, weight]
        if t == 0:
            pack[...] = jnp.concatenate(ones, axis=0).astype(BF)
        comb[t, 0] = jnp.concatenate(lefts, axis=0).T.astype(BF)
        comb[t, 1] = jnp.concatenate(rights, axis=0).T.astype(BF)

    def hidden(n):
        @pl.loop(0, HID // 256)
        def _(k):
            v = dot(rows[n], w[:, tile(k, 256)])
            h, a = v[0:80], v[80:160]
            s = jax.nn.sigmoid(h)
            hg = a * s * (1.0 + h * (1.0 - s))
            pair[n, :, tile(k, 256)] = jnp.concatenate([hg, h * s], axis=0).astype(BF)

    def receive(n):
        arrive(gx[n])

        @pl.loop(0, 2)
        def _(h):
            v = dot(undo[...], grecv[n - 1, :, :, tile(h, 256)].reshape(640, 256)).astype(BF)
            for i in range(4):
                rows[n - 1, :, pl.ds(pl.multiple_of(i * 512 + h * 256, 256), 256)] = v[i * 160 : (i + 1) * 160]

        hidden(n - 1)

    def forward_rows():
        @pl.loop(0, WIDE // 256)
        def _(n):
            at = tile(n, 256)
            top = dot(pack[...], xf[:, 0:TOK, at].reshape(wide, 256))
            low = dot(pack[...], xf[:, TOK : 2 * TOK, at].reshape(wide, 256))
            for j in range(NQ):
                cut = slice(j * SLOT, (j + 1) * SLOT)
                msg = jnp.concatenate([top[cut], low[cut]], axis=0).astype(BF)
                if j == 0:
                    frecv[0, :, at] = msg
                else:
                    fsend[j, :, at] = msg

        return [start(send(fsend.at[j], frecv.at[j], xs.at[5, j], xr.at[5, j], qdev(j))) for j in ORDER]

    for n in range(1, 5):
        prepare(n, places[n - 1], gated[n - 1])
        arrive(g[0])
        if n < 4:
            g[0] = gather(0, n + 1)
            gx[n] = dispatch(n)
            forward(n + 1)
        else:
            pack_single(4, 4, 1)
            gx[4] = send_single(4, 1)
            arrive(g[1])
            fx = forward_rows()
        if n == 1:
            slots(0)
            undo1[...] = order(10)
            slots(1)
            w_copy.wait()
        elif n == 2:
            arrive(gx[0])
            first[...] = dot(undo1[...], orecv[0].reshape(640, 256))
            receive(1)
        else:
            receive(n - 1)

    arrive(gx[4])
    last = dot(undo1[...], orecv[1].reshape(640, 256))
    for i in range(8):
        pieces = [v[i * 80 + h : i * 80 + h + 40] for h in (0, 40) for v in (first, last)]
        rows[3, :, i * 256 : (i + 1) * 256] = jnp.concatenate(pieces, axis=0).astype(BF)
    hidden(3)

    per = WIDE // PIECES

    def weight_part(owner, k):
        at = pl.ds(pl.multiple_of(owner * WIDE + k * per, per), per)
        return dot_tl(rows[:, :, at].reshape(640, per), pair[...].reshape(640, HID)).astype(BF)

    wcopies = []

    def other_half(k):
        wsend[k] = weight_part(1 - half, k)
        wcopies.append(start(send(wsend.at[k], wrecv.at[k], ds_.at[k], dr.at[k], {"dp": 1 - half})))

    other_half(0)
    def give_back(t, source):
        copies = []
        for h in range(2):
            unit = 2 * t + h

            @pl.loop(0, 2)
            def _(n):
                at = tile(n, 256)
                left = dot_t(source, w[pl.ds(pl.multiple_of(h * 512 + n * 256, 256), 256), :])
                right = dot_t(source, w[pl.ds(pl.multiple_of(WIDE + h * 512 + n * 256, 256), 256), :])
                for j in range(NQ):
                    cut = slice(j * SLOT, (j + 1) * SLOT)
                    msg = jnp.concatenate([left[cut], right[cut]], axis=0).astype(BF)
                    if j == 0:
                        rrecv[unit, 0, :, at] = msg
                    else:
                        rsend[unit, j, :, at] = msg

            copies.append([
                start(send(rsend.at[unit, j], rrecv.at[unit, j], bs.at[unit, j], br.at[unit, j], qdev(j)))
                for j in ORDER
            ])
        return copies

    a = iota((320, 320), 0)
    j8 = div(a, 40)
    a = a - j8 * 40
    n4 = div(a, 10)
    a = a - n4 * 10
    b2 = div(a, CAP)
    source = jnp.where(n4 < 3, n4 * 80 + j8 * 10 + a, 240 + b2 * 40 + j8 * CAP + (a - b2 * CAP))
    turn = jnp.where(iota((320, 320), 1) == source, 1.0, 0.0).astype(BF)
    b1 = give_back(1, dot(turn, pair[:, 0:80, :].reshape(320, HID)).astype(BF))

    for k in range(1, 4):
        other_half(k)

    arrive(fx)

    @pl.loop(0, WIDE // 256)
    def _(n):
        v = frecv[:, :, tile(n, 256)].astype(F32)
        frow[:, tile(n, 256)] = v[:, 0:SLOT].reshape(SLOT * NQ, 256).astype(BF)
        frow[:, pl.ds(pl.multiple_of(WIDE + n * 256, 256), 256)] = v[:, SLOT:].reshape(SLOT * NQ, 256).astype(BF)

    @pl.loop(0, HID // 256)
    def _(n):
        h = dot(frow[...], w[:, tile(n, 256)])
        fh[:, tile(n, 256)] = (h * jax.nn.sigmoid(h)).astype(BF)

    b0 = give_back(0, fh[...])
    for k in range(4, PIECES):
        other_half(k)

    def combine(u):
        @pl.loop(0, 2)
        def _(n):
            at = tile(n, 256)
            got = rrecv[u, :, :, at].reshape(2 * SLOT * NQ, 256)
            part[u, :, 0:TOK, at] = dot(comb[u // 2, 0], got).reshape(NY, TOK, 256)
            part[u, :, TOK : 2 * TOK, at] = dot(comb[u // 2, 1], got).reshape(NY, TOK, 256)

    r = {}

    def reduce_step(u, step):
        copies = []
        for way in range(2):
            if step == 1:
                cut = slice(way * TOK, (way + 1) * TOK)
                ysend[u, 0, way, cut] = part[u, 4, cut].astype(BF)
                where = pl.ds(way * TOK, TOK)
                a, b = ysend.at[u, 0, way, where], yrecv.at[u, 0, way, where]
            else:
                s = step - 1
                r[u][way].wait_recv()
                d = 5 - step if way == 0 else 3 + step
                if step == 2:
                    got = slice(way * TOK, (way + 1) * TOK)
                    rest = slice((1 - way) * TOK, (2 - way) * TOK)
                    ysend[u, s, way, got] = (part[u, d, got] + yrecv[u, 0, way, got].astype(F32)).astype(BF)
                    ysend[u, s, way, rest] = part[u, d, rest].astype(BF)
                else:
                    ysend[u, s, way] = (part[u, d] + yrecv[u, s - 1, way].astype(F32)).astype(BF)
                a, b = ysend.at[u, s, way], yrecv.at[u, s, way]
            copies.append(start(send(a, b, ys.at[u, step - 1, way], yr.at[u, step - 1, way], ydev(1 - 2 * way))))
        r[u] = copies

    pipes = {}

    def finish(u):
        arrive(r[u])
        total = part[u, 0] + yrecv[u, 3, 0].astype(F32) + yrecv[u, 3, 1].astype(F32)
        t, h = u // 2, u % 2
        for i in range(2):
            if t == 1:
                base = xsg[0, TOK : 2 * TOK, i * WIDE + h * 512 : i * WIDE + h * 512 + 512]
            else:
                base = xf[0, i * TOK : (i + 1) * TOK, h * 512 : h * 512 + 512]
            cut = slice(i * TOK, (i + 1) * TOK)
            out_send[u, cut] = (base.astype(F32) + total[cut]).astype(BF)
        to = (p + (3 if t == 1 else 1)) % 4
        pipes[u] = start(send(out_send.at[u], out_recv.at[u], ps.at[u], pr.at[u], {"pipe": to}))

    def own_half(k):
        wown[k] = weight_part(half, k)

    outs = []

    def place_out(src, dst):
        copy = pltpu.make_async_copy(src, dst, out_sem.at[len(outs)])
        copy.start()
        outs.append(copy)

    def sum_half(k):
        wcopies[k].wait_recv()
        wown[k] = (wown[k].astype(F32) + wrecv[k].astype(F32)).astype(BF)
        place_out(wown.at[k], wg_ref.at[pl.ds(k * per, per)])

    waits = {2: b1[0], 3: b1[1], 0: b0[0], 1: b0[1]}
    begun = {2: 0, 3: 2, 0: 4, 1: 6}
    pieces = list(range(PIECES))
    for tick in range(11):
        for u in (2, 3, 0, 1):
            step = tick - begun[u] + 1
            if step == 1:
                arrive(waits[u])
                combine(u)
            if 1 <= step <= 4:
                reduce_step(u, step)
            if step == 5:
                finish(u)
        for _ in range(2):
            if pieces:
                own_half(pieces.pop(0))
        if tick in (4, 6, 8, 9):
            sum_half((4, 6, 8, 9).index(tick))

    def take(u):
        pipes[u].wait_recv()
        out = prior_ref if u >= 2 else next_ref
        for i in range(2):
            place_out(out_recv.at[u, pl.ds(i * TOK, TOK)], out.at[:, pl.ds(i * WIDE + (u % 2) * 512, 512)])

    take(2)
    take(3)
    for k in range(4, PIECES):
        sum_half(k)
    take(0)
    take(1)
    for copy in outs:
        copy.wait()
    for copy in sent:
        copy.wait_send()


def finish_kernel(a, b, c, x, y, z, va, vb, vc, sems):
    pieces = [(c.at[pl.ds(i * 256, 256)], vc.at[i], z.at[pl.ds(i * 256, 256)]) for i in range(4)]
    pieces += [(a, va, x), (b, vb, y)]
    loads = [pltpu.make_async_copy(u, m, sems.at[0, i]) for i, (u, m, _) in enumerate(pieces)]
    stores = [pltpu.make_async_copy(m, o, sems.at[1, i]) for i, (_, m, o) in enumerate(pieces)]
    for copy in loads:
        copy.start()
    for load, store in zip(loads, stores):
        load.wait()
        store.start()
    for copy in stores:
        copy.wait()


def relay(rf, rb, gf, gb, s, o, f, w):
    vmem = pl.BlockSpec(memory_space=pltpu.VMEM)
    dma = pltpu.SemaphoreType.DMA
    v = pltpu.VMEM
    two = 2 * SLOT
    return pl.pallas_call(
        kernel,
        out_shape=(
            jax.ShapeDtypeStruct((TOK, D), BF),
            jax.ShapeDtypeStruct((TOK, D), BF),
            jax.ShapeDtypeStruct((D // 2, HID), BF),
        ),
        in_specs=[vmem] * 4 + [pl.BlockSpec(memory_space=pl.ANY)] * 4,
        out_specs=(pl.BlockSpec(memory_space=pl.ANY),) * 3,
        scratch_shapes=[
            v((D, HID), BF),
            v((NY, 8, 128), F32),
            v((NY, 2 * TOK, D), BF),
            v((NY, 2 * TOK, WIDE), BF),
            v((3, NQ, two, 512), BF),
            v((3, NQ, two, 512), BF),
            v((2, NQ, two, 256), BF),
            v((2, NQ, two, 256), BF),
            v((640, 256), F32),
            v((NQ, two, WIDE), BF),
            v((NQ, two, WIDE), BF),
            v((4, NQ, two, 512), BF),
            v((4, NQ, two, 512), BF),
            v((4, 160, D), BF),
            v((4, 160, HID), BF),
            v((SLOT * NQ, D), BF),
            v((SLOT * NQ, HID), BF),
            v((5, 640, 512), BF),
            v((5, 640, 128), F32),
            v((640, 640), BF),
            v((640, 640), BF),
            v((SLOT * NQ, NY * TOK), BF),
            v((2, 2, NY * TOK, two * NQ), BF),
            v((4, NY, 2 * TOK, 512), F32),
            v((4, 4, 2, 2 * TOK, 512), BF),
            v((4, 4, 2, 2 * TOK, 512), BF),
            v((4, 2 * TOK, 512), BF),
            v((4, 2 * TOK, 512), BF),
            v((PIECES, WIDE // PIECES, HID), BF),
            v((PIECES, WIDE // PIECES, HID), BF),
            v((PIECES, WIDE // PIECES, HID), BF),
            dma,
            dma((4,)),
            dma((PIECES + 8,)),
            dma((NY,)), dma((NY,)),
            dma((2, 4, 2)), dma((2, 4, 2)),
            dma((6, NQ)), dma((6, NQ)),
            dma((4, NQ)), dma((4, NQ)),
            dma((4, 4, 2)), dma((4, 4, 2)),
            dma((PIECES,)), dma((PIECES,)),
            dma((4,)), dma((4,)),
        ],
        compiler_params=pltpu.CompilerParams(
            collective_id=0, has_side_effects=True, vmem_limit_bytes=58 << 20
        ),
        cost_estimate=pl.CostEstimate(flops=8 * 10**9, bytes_accessed=10**7, transcendentals=10**6),
        name="relay",
    )(rf, rb, gf, gb, s, o, f, w)


def on_device(section_inputs, saved_inputs, output_grads, forward_routes, backward_routes,
              forward_gates, backward_gates, expert_weights):
    outs = relay(
        forward_routes[0].T, backward_routes[0].T, forward_gates[0].T, backward_gates[0].T,
        saved_inputs[0], output_grads[0], section_inputs[0], expert_weights[0, 0],
    )
    anywhere = pl.BlockSpec(memory_space=pl.ANY)
    after, prior, wg = pl.pallas_call(
        finish_kernel,
        out_shape=[jax.ShapeDtypeStruct(v.shape, v.dtype) for v in outs],
        in_specs=[anywhere] * 3,
        out_specs=[anywhere] * 3,
        scratch_shapes=[
            pltpu.VMEM((TOK, D), BF),
            pltpu.VMEM((TOK, D), BF),
            pltpu.VMEM((4, 256, HID), BF),
            pltpu.SemaphoreType.DMA((2, 6)),
        ],
        name="place",
    )(*outs)
    return after[None], prior[None], wg[None, None]


def solution(mesh):
    placed = P("pipe", ("expert", "dp"), None)
    return jax.shard_map(
        on_device,
        mesh=mesh,
        in_specs=(placed,) * 7 + (P("pipe", "expert", None, None),),
        out_specs=(placed, placed, P("pipe", "expert", "dp", None)),
        check_vma=False,
    )
```

```python
import functools

import jax
import jax.numpy as jnp
from jax import lax
from jax.experimental import pallas as pl
from jax.experimental.pallas import tpu as pltpu
from jax.sharding import PartitionSpec as P

MESH = pl.DeviceIdType.MESH
BF = jnp.bfloat16
F32 = jnp.float32
TOK = 32
CAP = 5
NY = 8
NQ = 8
WIDE = 1024
PAIRS = ((1, 7), (2, 6), (3, 5))
SLOT = NY * CAP
D = 2048
HID = 768
PIECES = 8
ORDER = (4, 5, 2, 3, 6, 7, 1)


def dot(a, b):
    return jnp.dot(a, b, preferred_element_type=F32)


def dot_t(a, b):
    return lax.dot_general(a, b, (((1,), (1,)), ((), ())), preferred_element_type=F32)


def dot_tl(a, b):
    return lax.dot_general(a, b, (((0,), (0,)), ((), ())), preferred_element_type=F32)


def tile(i, n):
    return pl.ds(pl.multiple_of(i * n, n), n)


def div(v, n):
    return lax.shift_right_logical(v * (-(-65536 // n)), 16)


def iota(shape, axis):
    return lax.broadcasted_iota(jnp.int32, shape, axis)


def kernel(
    rf_ref, rb_ref, gf_ref, gb_ref, s_hbm, o_hbm, f_hbm, w_hbm,
    next_ref, prior_ref, wg_ref,
    w, metas, xsg, xf, gsend, grecv, osend, orecv, first, fsend, frecv, rsend, rrecv, rows, pair, frow, fh,
    big, scale, undo, undo1, pack, comb, part, ysend, yrecv, out_send, out_recv, wsend, wrecv, wown,
    w_sem, in_sem, out_sem, ms, mr, gs, gr, xs, xr, bs, br, ys, yr, ds_, dr, ps, pr,
):
    e = lax.axis_index("expert")
    p = lax.axis_index("pipe")
    half = lax.axis_index("dp")
    y, q = e // NQ, e % NQ
    x, c = q // 2, q % 2

    def ydev(k):
        return {"expert": ((y + k + NY) % NY) * NQ + q}

    def qdev(j):
        jx, jc = j // 2, j % 2
        other = ((x // 2 + jx // 2) % 2) * 2 + (x % 2 + jx % 2) % 2
        return {"expert": y * NQ + other * 2 + (c + jc) % 2}

    def send(src, dst, ssem, rsem, dev):
        return pltpu.make_async_remote_copy(
            src_ref=src, dst_ref=dst, send_sem=ssem, recv_sem=rsem, device_id=dev, device_id_type=MESH
        )

    sent = []

    def start(copy):
        copy.start()
        sent.append(copy)
        return copy

    def arrive(copies):
        for copy in copies:
            copy.wait_recv()

    barrier = pltpu.get_barrier_semaphore()
    friends = [ydev(k) for k in range(1, NY)] + [qdev(j) for j in range(1, NQ)]
    friends += [{"dp": 1 - half}, {"pipe": (p + 1) % 4}, {"pipe": (p + 3) % 4}]
    for dev in friends:
        pl.semaphore_signal(barrier, inc=1, device_id=dev, device_id_type=MESH)

    inputs = [
        pltpu.make_async_copy(u, v, in_sem.at[i])
        for i, (u, v) in enumerate((
            (s_hbm, xsg.at[0, pl.ds(0, TOK)]),
            (o_hbm, xsg.at[0, pl.ds(TOK, TOK)]),
            (f_hbm.at[:, pl.ds(0, WIDE)], xf.at[0, pl.ds(0, TOK)]),
            (f_hbm.at[:, pl.ds(WIDE, WIDE)], xf.at[0, pl.ds(TOK, TOK)]),
        ))
    ]
    for copy in inputs:
        copy.start()
    w_copy = pltpu.make_async_copy(w_hbm, w, w_sem)
    w_copy.start()

    metas[0] = jnp.concatenate(
        [rf_ref[...].astype(F32), rb_ref[...].astype(F32), gf_ref[...], gb_ref[...]], axis=1
    )

    lane = div(iota((8, 128), 1), TOK)

    def lanes_of(kind, blocks):
        v = None
        for b, d in enumerate(blocks):
            shift = ((b - kind) * TOK) % 128
            u = metas[d]
            if shift:
                u = pltpu.roll(u, shift, 1)
            v = u if v is None else jnp.where(lane == b, u, v)
        return v

    expert = (y * NQ + jnp.bitwise_xor(iota((NQ, 128), 0), q)).astype(F32)

    def routed(t, blocks):
        routes, gates = lanes_of(t, blocks), lanes_of(2 + t, blocks)
        mark = jnp.zeros((NQ, 128), F32)
        gate = jnp.zeros((NQ, 128), F32)
        for k in range(8):
            same = routes[k : k + 1, :] == expert
            mark = mark + jnp.where(same, 1.0, 0.0)
            gate = gate + jnp.where(same, gates[k : k + 1, :], 0.0)
        return mark, gate

    r2, l2 = iota((128, 128), 0), iota((128, 128), 1)
    earlier = jnp.where((div(r2, TOK) == div(l2, TOK)) & (r2 < l2), 1.0, 0.0).astype(BF)

    def places_of(marks):
        return jnp.where(marks > 0.5, dot(marks.astype(BF), earlier), -1.0)

    spread = jnp.where(iota((640, NQ), 1) == div(iota((640, NQ), 0), 80), 1.0, 0.0)

    def prepare(n, spot, gate):
        r, l = iota((640, 128), 0), iota((640, 128), 1)
        r = r - div(r, 80) * 80
        l64 = div(l, 64)
        single = n in (0, 4)
        count = 10 if single else 20
        part_of = div(r, count)
        r = r - part_of * count
        tensor = div(r, count // 2)
        r = r - tensor * (count // 2)
        fits = div(l, TOK) - 2 * l64 == tensor
        if not single:
            b2 = div(r, CAP)
            fits = fits & (l64 == b2)
            r = r - b2 * CAP
        want = jnp.where(fits, r, -2).astype(F32)
        where = dot(spread.astype(BF), spot.astype(BF))
        hit = jnp.where(where == want, 1.0, 0.0)
        gate = jnp.dot(spread, gate, preferred_element_type=F32, precision=lax.Precision.HIGHEST)
        counted = jnp.where(l64 == 0, hit * gate, 0.0) if single else hit * gate
        total = jnp.sum(counted, axis=1, keepdims=True)
        scale[n] = jnp.where(tensor == 0, 1.0, jnp.broadcast_to(total, (640, 128)))
        for i in range(4):
            here = part_of == (2 * i + l64 if single else i)
            big[n, :, i * 128 : (i + 1) * 128] = jnp.where(here, hit, 0.0).astype(BF)

    def pack_single(n, d, k):
        stack = [xsg[d, :, i * 256 : (i + 1) * 256] for i in range(8)]
        v = dot(big[n], jnp.concatenate(stack, axis=0)) * scale[n, :, 0:1]
        v = v.astype(BF).reshape(NQ, 80, 256)
        orecv[k, 0] = v[0]
        osend[k, 1:] = v[1:]

    def send_single(n, k):
        return [start(send(osend.at[k, j], orecv.at[k, j], xs.at[n, j], xr.at[n, j], qdev(j))) for j in ORDER]

    mark, gate = routed(1, (0, 0, 0, 0))
    prepare(0, places_of(mark), gate)
    inputs[0].wait()
    inputs[1].wait()
    pack_single(0, 0, 0)

    pl.semaphore_wait(barrier, len(friends))

    def gather(i, step):
        buf = (xsg, xf)[i]
        copies = []
        for way in range(2):
            src, dst = ((NY - step + 1) % NY, NY - step) if way == 0 else (step - 1, step)
            if step < 4:
                a, b = buf.at[src], buf.at[dst]
            else:
                cut = pl.ds(way * TOK, TOK)
                a, b = buf.at[src, cut], buf.at[dst, cut]
            copies.append(start(send(a, b, gs.at[i, step - 1, way], gr.at[i, step - 1, way], ydev(1 - 2 * way))))
        return copies

    for k in (1, 7, 2, 6, 3, 5, 4):
        start(send(metas.at[0], metas.at[NY - k], ms.at[k], mr.at[NY - k], ydev(k)))
    g = {0: gather(0, 1)}

    gx = {0: send_single(0, 0)}
    inputs[2].wait()
    inputs[3].wait()
    g[1] = gather(1, 1)

    def order(width):
        m, a = iota((640, 640), 1), iota((640, 640), 0)
        i = div(a, 8 * width)
        a = a - i * 8 * width
        tensor = div(a, 4 * width)
        a = a - tensor * 4 * width
        j = div(a, width // 2)
        a = a - j * (width // 2)
        return jnp.where(m == j * 80 + i * width + tensor * (width // 2) + a, 1.0, 0.0).astype(BF)

    undo[...] = order(20)

    for k in range(1, NY):
        send(metas.at[0], metas.at[k], ms.at[k], mr.at[k], ydev(k)).wait_recv()

    sets = [(1, (u, u, v, v)) for u, v in PAIRS] + [(1, (4, 4, 4, 4))]
    sets += [(t, tuple(range(4 * h, 4 * h + 4))) for t in range(2) for h in range(2)]
    found = [routed(*one) for one in sets]
    place = places_of(jnp.concatenate([one[0] for one in found], axis=0))
    places = [place[n * NQ : (n + 1) * NQ] for n in range(8)]
    gated = [one[1] for one in found]

    def dispatch(n):
        @pl.loop(0, 2)
        def _(h):
            stack = [
                xsg[d, :, pl.ds(pl.multiple_of(i * 512 + h * 256, 256), 256)]
                for i in range(4) for d in PAIRS[n - 1]
            ]
            v = dot(big[n], jnp.concatenate(stack, axis=0)) * scale[n, :, 0:1]
            v = v.astype(BF).reshape(NQ, 80, 256)
            grecv[n - 1, 0, :, tile(h, 256)] = v[0]
            gsend[n - 1, 1:, :, tile(h, 256)] = v[1:]

        return [
            start(send(gsend.at[n - 1, j], grecv.at[n - 1, j], xs.at[n, j], xr.at[n, j], qdev(j))) for j in ORDER
        ]

    def forward(step):
        arrive(g[1])
        g[1] = gather(1, step)

    wide = NY * TOK

    def full(v, t):
        return jnp.concatenate([v[4 + 2 * t], v[5 + 2 * t]], axis=1)

    zeros = jnp.zeros((SLOT, wide), F32)

    def slots(t):
        rr, ll = iota((SLOT, wide), 0), iota((SLOT, wide), 1)
        block = div(rr, CAP)
        d = block
        if t == 1:
            up = div(block, 2)
            d = jnp.where(block == 2 * up, up + 1, NY - 1 - up)
            d = jnp.where(block == 6, 0, jnp.where(block == 7, 4, d))
        target = jnp.where(div(ll, TOK) == d, rr - block * CAP, -2).astype(F32)
        ones, lefts, rights = [], [], []
        spot, gate = full(places, t), full(gated, t)
        for j in range(NQ):
            hit = jnp.where(spot[j : j + 1, :] == target, 1.0, 0.0)
            weight = hit * gate[j : j + 1, :] if t == 0 else hit
            ones.append(hit)
            lefts += [weight, zeros]
            rights += [zeros, weight]
        if t == 0:
            pack[...] = jnp.concatenate(ones, axis=0).astype(BF)
        comb[t, 0] = jnp.concatenate(lefts, axis=0).T.astype(BF)
        comb[t, 1] = jnp.concatenate(rights, axis=0).T.astype(BF)

    def hidden(n):
        @pl.loop(0, HID // 256)
        def _(k):
            v = dot(rows[n], w[:, tile(k, 256)])
            h, a = v[0:80], v[80:160]
            s = jax.nn.sigmoid(h)
            hg = a * s * (1.0 + h * (1.0 - s))
            pair[n, :, tile(k, 256)] = jnp.concatenate([hg, h * s], axis=0).astype(BF)

    def receive(n):
        arrive(gx[n])

        @pl.loop(0, 2)
        def _(h):
            v = dot(undo[...], grecv[n - 1, :, :, tile(h, 256)].reshape(640, 256)).astype(BF)
            for i in range(4):
                rows[n - 1, :, pl.ds(pl.multiple_of(i * 512 + h * 256, 256), 256)] = v[i * 160 : (i + 1) * 160]

        hidden(n - 1)

    def forward_rows():
        @pl.loop(0, WIDE // 256)
        def _(n):
            at = tile(n, 256)
            top = dot(pack[...], xf[:, 0:TOK, at].reshape(wide, 256))
            low = dot(pack[...], xf[:, TOK : 2 * TOK, at].reshape(wide, 256))
            for j in range(NQ):
                cut = slice(j * SLOT, (j + 1) * SLOT)
                msg = jnp.concatenate([top[cut], low[cut]], axis=0).astype(BF)
                if j == 0:
                    frecv[0, :, at] = msg
                else:
                    fsend[j, :, at] = msg

        return [start(send(fsend.at[j], frecv.at[j], xs.at[5, j], xr.at[5, j], qdev(j))) for j in ORDER]

    for n in range(1, 5):
        prepare(n, places[n - 1], gated[n - 1])
        arrive(g[0])
        if n < 4:
            g[0] = gather(0, n + 1)
            gx[n] = dispatch(n)
            forward(n + 1)
        else:
            pack_single(4, 4, 1)
            gx[4] = send_single(4, 1)
        if n == 1:
            slots(0)
            undo1[...] = order(10)
            slots(1)
            w_copy.wait()
        elif n == 2:
            arrive(gx[0])
            first[...] = dot(undo1[...], orecv[0].reshape(640, 256))
            receive(1)
        else:
            receive(n - 1)

    arrive(gx[4])
    last = dot(undo1[...], orecv[1].reshape(640, 256))
    for i in range(8):
        pieces = [v[i * 80 + h : i * 80 + h + 40] for h in (0, 40) for v in (first, last)]
        rows[3, :, i * 256 : (i + 1) * 256] = jnp.concatenate(pieces, axis=0).astype(BF)
    hidden(3)

    per = WIDE // PIECES

    def weight_part(owner, k):
        at = pl.ds(pl.multiple_of(owner * WIDE + k * per, per), per)
        return dot_tl(rows[:, :, at].reshape(640, per), pair[...].reshape(640, HID)).astype(BF)

    wcopies = []

    def other_half(k):
        wsend[k] = weight_part(1 - half, k)
        wcopies.append(start(send(wsend.at[k], wrecv.at[k], ds_.at[k], dr.at[k], {"dp": 1 - half})))

    other_half(0)
    arrive(g[1])
    fx = forward_rows()
    def give_back(t, source):
        copies = []
        for h in range(2):
            unit = 2 * t + h

            @pl.loop(0, 2)
            def _(n):
                at = tile(n, 256)
                left = dot_t(source, w[pl.ds(pl.multiple_of(h * 512 + n * 256, 256), 256), :])
                right = dot_t(source, w[pl.ds(pl.multiple_of(WIDE + h * 512 + n * 256, 256), 256), :])
                for j in range(NQ):
                    cut = slice(j * SLOT, (j + 1) * SLOT)
                    msg = jnp.concatenate([left[cut], right[cut]], axis=0).astype(BF)
                    if j == 0:
                        rrecv[unit, 0, :, at] = msg
                    else:
                        rsend[unit, j, :, at] = msg

            copies.append([
                start(send(rsend.at[unit, j], rrecv.at[unit, j], bs.at[unit, j], br.at[unit, j], qdev(j)))
                for j in ORDER
            ])
        return copies

    a = iota((320, 320), 0)
    j8 = div(a, 40)
    a = a - j8 * 40
    n4 = div(a, 10)
    a = a - n4 * 10
    b2 = div(a, CAP)
    source = jnp.where(n4 < 3, n4 * 80 + j8 * 10 + a, 240 + b2 * 40 + j8 * CAP + (a - b2 * CAP))
    turn = jnp.where(iota((320, 320), 1) == source, 1.0, 0.0).astype(BF)
    b1 = give_back(1, dot(turn, pair[:, 0:80, :].reshape(320, HID)).astype(BF))

    for k in range(1, 3):
        other_half(k)

    arrive(fx)

    @pl.loop(0, WIDE // 256)
    def _(n):
        v = frecv[:, :, tile(n, 256)].astype(F32)
        frow[:, tile(n, 256)] = v[:, 0:SLOT].reshape(SLOT * NQ, 256).astype(BF)
        frow[:, pl.ds(pl.multiple_of(WIDE + n * 256, 256), 256)] = v[:, SLOT:].reshape(SLOT * NQ, 256).astype(BF)

    @pl.loop(0, HID // 256)
    def _(n):
        h = dot(frow[...], w[:, tile(n, 256)])
        fh[:, tile(n, 256)] = (h * jax.nn.sigmoid(h)).astype(BF)

    b0 = give_back(0, fh[...])
    for k in range(3, 4):
        other_half(k)

    def combine(u):
        @pl.loop(0, 2)
        def _(n):
            at = tile(n, 256)
            got = rrecv[u, :, :, at].reshape(2 * SLOT * NQ, 256)
            part[u, :, 0:TOK, at] = dot(comb[u // 2, 0], got).reshape(NY, TOK, 256)
            part[u, :, TOK : 2 * TOK, at] = dot(comb[u // 2, 1], got).reshape(NY, TOK, 256)

    r = {}

    def reduce_step(u, step):
        copies = []
        for way in range(2):
            if step == 1:
                cut = slice(way * TOK, (way + 1) * TOK)
                ysend[u, 0, way, cut] = part[u, 4, cut].astype(BF)
                where = pl.ds(way * TOK, TOK)
                a, b = ysend.at[u, 0, way, where], yrecv.at[u, 0, way, where]
            else:
                s = step - 1
                r[u][way].wait_recv()
                d = 5 - step if way == 0 else 3 + step
                if step == 2:
                    got = slice(way * TOK, (way + 1) * TOK)
                    rest = slice((1 - way) * TOK, (2 - way) * TOK)
                    ysend[u, s, way, got] = (part[u, d, got] + yrecv[u, 0, way, got].astype(F32)).astype(BF)
                    ysend[u, s, way, rest] = part[u, d, rest].astype(BF)
                else:
                    ysend[u, s, way] = (part[u, d] + yrecv[u, s - 1, way].astype(F32)).astype(BF)
                a, b = ysend.at[u, s, way], yrecv.at[u, s, way]
            copies.append(start(send(a, b, ys.at[u, step - 1, way], yr.at[u, step - 1, way], ydev(1 - 2 * way))))
        r[u] = copies

    pipes = {}

    def finish(u):
        arrive(r[u])
        total = part[u, 0] + yrecv[u, 3, 0].astype(F32) + yrecv[u, 3, 1].astype(F32)
        t, h = u // 2, u % 2
        for i in range(2):
            if t == 1:
                base = xsg[0, TOK : 2 * TOK, i * WIDE + h * 512 : i * WIDE + h * 512 + 512]
            else:
                base = xf[0, i * TOK : (i + 1) * TOK, h * 512 : h * 512 + 512]
            cut = slice(i * TOK, (i + 1) * TOK)
            out_send[u, cut] = (base.astype(F32) + total[cut]).astype(BF)
        to = (p + (3 if t == 1 else 1)) % 4
        pipes[u] = start(send(out_send.at[u], out_recv.at[u], ps.at[u], pr.at[u], {"pipe": to}))

    def own_half(k):
        wown[k] = weight_part(half, k)

    outs = []

    def place_out(src, dst):
        copy = pltpu.make_async_copy(src, dst, out_sem.at[len(outs)])
        copy.start()
        outs.append(copy)

    def sum_half(k):
        wcopies[k].wait_recv()
        wown[k] = (wown[k].astype(F32) + wrecv[k].astype(F32)).astype(BF)
        place_out(wown.at[k], wg_ref.at[pl.ds(k * per, per)])

    waits = {2: b1[0], 3: b1[1], 0: b0[0], 1: b0[1]}
    begun = {2: 0, 3: 2, 0: 4, 1: 6}
    pieces = list(range(PIECES))
    later = (1, 3, 5, 7)
    for tick in range(11):
        for u in (2, 3, 0, 1):
            step = tick - begun[u] + 1
            if step == 1:
                arrive(waits[u])
                combine(u)
            if 1 <= step <= 4:
                reduce_step(u, step)
            if step == 5:
                finish(u)
        for _ in range(2):
            if pieces:
                own_half(pieces.pop(0))
        if tick in later:
            other_half(4 + later.index(tick))
        if tick in (4, 6, 8, 9):
            sum_half((4, 6, 8, 9).index(tick))

    def take(u):
        pipes[u].wait_recv()
        out = prior_ref if u >= 2 else next_ref
        for i in range(2):
            place_out(out_recv.at[u, pl.ds(i * TOK, TOK)], out.at[:, pl.ds(i * WIDE + (u % 2) * 512, 512)])

    take(2)
    take(3)
    for k in range(4, PIECES):
        sum_half(k)
    take(0)
    take(1)
    for copy in outs:
        copy.wait()
    for copy in sent:
        copy.wait_send()


def finish_kernel(a, b, c, x, y, z, va, vb, vc, sems):
    pieces = [(c.at[pl.ds(i * 256, 256)], vc.at[i], z.at[pl.ds(i * 256, 256)]) for i in range(4)]
    pieces += [(a, va, x), (b, vb, y)]
    loads = [pltpu.make_async_copy(u, m, sems.at[0, i]) for i, (u, m, _) in enumerate(pieces)]
    stores = [pltpu.make_async_copy(m, o, sems.at[1, i]) for i, (_, m, o) in enumerate(pieces)]
    for copy in loads:
        copy.start()
    for load, store in zip(loads, stores):
        load.wait()
        store.start()
    for copy in stores:
        copy.wait()


def relay(rf, rb, gf, gb, s, o, f, w):
    vmem = pl.BlockSpec(memory_space=pltpu.VMEM)
    dma = pltpu.SemaphoreType.DMA
    v = pltpu.VMEM
    two = 2 * SLOT
    return pl.pallas_call(
        kernel,
        out_shape=(
            jax.ShapeDtypeStruct((TOK, D), BF),
            jax.ShapeDtypeStruct((TOK, D), BF),
            jax.ShapeDtypeStruct((D // 2, HID), BF),
        ),
        in_specs=[vmem] * 4 + [pl.BlockSpec(memory_space=pl.ANY)] * 4,
        out_specs=(pl.BlockSpec(memory_space=pl.ANY),) * 3,
        scratch_shapes=[
            v((D, HID), BF),
            v((NY, 8, 128), F32),
            v((NY, 2 * TOK, D), BF),
            v((NY, 2 * TOK, WIDE), BF),
            v((3, NQ, two, 512), BF),
            v((3, NQ, two, 512), BF),
            v((2, NQ, two, 256), BF),
            v((2, NQ, two, 256), BF),
            v((640, 256), F32),
            v((NQ, two, WIDE), BF),
            v((NQ, two, WIDE), BF),
            v((4, NQ, two, 512), BF),
            v((4, NQ, two, 512), BF),
            v((4, 160, D), BF),
            v((4, 160, HID), BF),
            v((SLOT * NQ, D), BF),
            v((SLOT * NQ, HID), BF),
            v((5, 640, 512), BF),
            v((5, 640, 128), F32),
            v((640, 640), BF),
            v((640, 640), BF),
            v((SLOT * NQ, NY * TOK), BF),
            v((2, 2, NY * TOK, two * NQ), BF),
            v((4, NY, 2 * TOK, 512), F32),
            v((4, 4, 2, 2 * TOK, 512), BF),
            v((4, 4, 2, 2 * TOK, 512), BF),
            v((4, 2 * TOK, 512), BF),
            v((4, 2 * TOK, 512), BF),
            v((PIECES, WIDE // PIECES, HID), BF),
            v((PIECES, WIDE // PIECES, HID), BF),
            v((PIECES, WIDE // PIECES, HID), BF),
            dma,
            dma((4,)),
            dma((PIECES + 8,)),
            dma((NY,)), dma((NY,)),
            dma((2, 4, 2)), dma((2, 4, 2)),
            dma((6, NQ)), dma((6, NQ)),
            dma((4, NQ)), dma((4, NQ)),
            dma((4, 4, 2)), dma((4, 4, 2)),
            dma((PIECES,)), dma((PIECES,)),
            dma((4,)), dma((4,)),
        ],
        compiler_params=pltpu.CompilerParams(
            collective_id=0, has_side_effects=True, vmem_limit_bytes=58 << 20
        ),
        cost_estimate=pl.CostEstimate(flops=8 * 10**9, bytes_accessed=10**7, transcendentals=10**6),
        name="relay",
    )(rf, rb, gf, gb, s, o, f, w)


def on_device(section_inputs, saved_inputs, output_grads, forward_routes, backward_routes,
              forward_gates, backward_gates, expert_weights):
    outs = relay(
        forward_routes[0].T, backward_routes[0].T, forward_gates[0].T, backward_gates[0].T,
        saved_inputs[0], output_grads[0], section_inputs[0], expert_weights[0, 0],
    )
    anywhere = pl.BlockSpec(memory_space=pl.ANY)
    after, prior, wg = pl.pallas_call(
        finish_kernel,
        out_shape=[jax.ShapeDtypeStruct(v.shape, v.dtype) for v in outs],
        in_specs=[anywhere] * 3,
        out_specs=[anywhere] * 3,
        scratch_shapes=[
            pltpu.VMEM((TOK, D), BF),
            pltpu.VMEM((TOK, D), BF),
            pltpu.VMEM((4, 256, HID), BF),
            pltpu.SemaphoreType.DMA((2, 6)),
        ],
        name="place",
    )(*outs)
    return after[None], prior[None], wg[None, None]


def solution(mesh):
    placed = P("pipe", ("expert", "dp"), None)
    return jax.shard_map(
        on_device,
        mesh=mesh,
        in_specs=(placed,) * 7 + (P("pipe", "expert", None, None),),
        out_specs=(placed, placed, P("pipe", "expert", "dp", None)),
        check_vma=False,
    )
```

```python
import functools

import jax
import jax.numpy as jnp
from jax import lax
from jax.experimental import pallas as pl
from jax.experimental.pallas import tpu as pltpu
from jax.sharding import PartitionSpec as P

MESH = pl.DeviceIdType.MESH
BF = jnp.bfloat16
F32 = jnp.float32
TOK = 32
CAP = 5
NY = 8
NQ = 8
WIDE = 1024
PAIRS = ((1, 7), (2, 6), (3, 5))
SLOT = NY * CAP
D = 2048
HID = 768
PIECES = 8
ORDER = (4, 5, 2, 3, 6, 7, 1)


def dot(a, b):
    return jnp.dot(a, b, preferred_element_type=F32)


def dot_t(a, b):
    return lax.dot_general(a, b, (((1,), (1,)), ((), ())), preferred_element_type=F32)


def dot_tl(a, b):
    return lax.dot_general(a, b, (((0,), (0,)), ((), ())), preferred_element_type=F32)


def tile(i, n):
    return pl.ds(pl.multiple_of(i * n, n), n)


def div(v, n):
    return lax.shift_right_logical(v * (-(-65536 // n)), 16)


def iota(shape, axis):
    return lax.broadcasted_iota(jnp.int32, shape, axis)


def kernel(
    rf_ref, rb_ref, gf_ref, gb_ref, s_hbm, o_hbm, f_hbm, w_hbm,
    next_ref, prior_ref, wg_ref,
    w, metas, xsg, xf, gsend, grecv, osend, orecv, first, fsend, frecv, rsend, rrecv, rows, pair, frow, fh,
    big, scale, undo, undo1, pack, comb, part, ysend, yrecv, out_send, out_recv, wsend, wrecv, wown,
    w_sem, in_sem, out_sem, ms, mr, gs, gr, xs, xr, bs, br, ys, yr, ds_, dr, ps, pr,
):
    e = lax.axis_index("expert")
    p = lax.axis_index("pipe")
    half = lax.axis_index("dp")
    y, q = e // NQ, e % NQ
    x, c = q // 2, q % 2

    def ydev(k):
        return {"expert": ((y + k + NY) % NY) * NQ + q}

    def qdev(j):
        jx, jc = j // 2, j % 2
        other = ((x // 2 + jx // 2) % 2) * 2 + (x % 2 + jx % 2) % 2
        return {"expert": y * NQ + other * 2 + (c + jc) % 2}

    def send(src, dst, ssem, rsem, dev):
        return pltpu.make_async_remote_copy(
            src_ref=src, dst_ref=dst, send_sem=ssem, recv_sem=rsem, device_id=dev, device_id_type=MESH
        )

    sent = []

    def start(copy):
        copy.start()
        sent.append(copy)
        return copy

    def arrive(copies):
        for copy in copies:
            copy.wait_recv()

    barrier = pltpu.get_barrier_semaphore()
    friends = [ydev(k) for k in range(1, NY)] + [qdev(j) for j in range(1, NQ)]
    friends += [{"dp": 1 - half}, {"pipe": (p + 1) % 4}, {"pipe": (p + 3) % 4}]
    for dev in friends:
        pl.semaphore_signal(barrier, inc=1, device_id=dev, device_id_type=MESH)

    inputs = [
        pltpu.make_async_copy(u, v, in_sem.at[i])
        for i, (u, v) in enumerate((
            (s_hbm, xsg.at[0, pl.ds(0, TOK)]),
            (o_hbm, xsg.at[0, pl.ds(TOK, TOK)]),
            (f_hbm.at[:, pl.ds(0, WIDE)], xf.at[0, pl.ds(0, TOK)]),
            (f_hbm.at[:, pl.ds(WIDE, WIDE)], xf.at[0, pl.ds(TOK, TOK)]),
        ))
    ]
    for copy in inputs:
        copy.start()
    w_copy = pltpu.make_async_copy(w_hbm, w, w_sem)
    w_copy.start()

    metas[0] = jnp.concatenate(
        [rf_ref[...].astype(F32), rb_ref[...].astype(F32), gf_ref[...], gb_ref[...]], axis=1
    )

    lane = div(iota((8, 128), 1), TOK)

    def lanes_of(kind, blocks):
        v = None
        for b, d in enumerate(blocks):
            shift = ((b - kind) * TOK) % 128
            u = metas[d]
            if shift:
                u = pltpu.roll(u, shift, 1)
            v = u if v is None else jnp.where(lane == b, u, v)
        return v

    expert = (y * NQ + jnp.bitwise_xor(iota((NQ, 128), 0), q)).astype(F32)

    def routed(t, blocks):
        routes, gates = lanes_of(t, blocks), lanes_of(2 + t, blocks)
        mark = jnp.zeros((NQ, 128), F32)
        gate = jnp.zeros((NQ, 128), F32)
        for k in range(8):
            same = routes[k : k + 1, :] == expert
            mark = mark + jnp.where(same, 1.0, 0.0)
            gate = gate + jnp.where(same, gates[k : k + 1, :], 0.0)
        return mark, gate

    r2, l2 = iota((128, 128), 0), iota((128, 128), 1)
    earlier = jnp.where((div(r2, TOK) == div(l2, TOK)) & (r2 < l2), 1.0, 0.0).astype(BF)

    def places_of(marks):
        return jnp.where(marks > 0.5, dot(marks.astype(BF), earlier), -1.0)

    spread = jnp.where(iota((640, NQ), 1) == div(iota((640, NQ), 0), 80), 1.0, 0.0)

    def prepare(n, spot, gate):
        r, l = iota((640, 128), 0), iota((640, 128), 1)
        r = r - div(r, 80) * 80
        l64 = div(l, 64)
        single = n in (0, 4)
        count = 10 if single else 20
        part_of = div(r, count)
        r = r - part_of * count
        tensor = div(r, count // 2)
        r = r - tensor * (count // 2)
        fits = div(l, TOK) - 2 * l64 == tensor
        if not single:
            b2 = div(r, CAP)
            fits = fits & (l64 == b2)
            r = r - b2 * CAP
        want = jnp.where(fits, r, -2).astype(F32)
        where = dot(spread.astype(BF), spot.astype(BF))
        hit = jnp.where(where == want, 1.0, 0.0)
        gate = jnp.dot(spread, gate, preferred_element_type=F32, precision=lax.Precision.HIGHEST)
        counted = jnp.where(l64 == 0, hit * gate, 0.0) if single else hit * gate
        total = jnp.sum(counted, axis=1, keepdims=True)
        scale[n] = jnp.where(tensor == 0, 1.0, jnp.broadcast_to(total, (640, 128)))
        for i in range(4):
            here = part_of == (2 * i + l64 if single else i)
            big[n, :, i * 128 : (i + 1) * 128] = jnp.where(here, hit, 0.0).astype(BF)

    def pack_single(n, d, k):
        stack = [xsg[d, :, i * 256 : (i + 1) * 256] for i in range(8)]
        v = dot(big[n], jnp.concatenate(stack, axis=0)) * scale[n, :, 0:1]
        v = v.astype(BF).reshape(NQ, 80, 256)
        orecv[k, 0] = v[0]
        osend[k, 1:] = v[1:]

    def send_single(n, k):
        return [start(send(osend.at[k, j], orecv.at[k, j], xs.at[n, j], xr.at[n, j], qdev(j))) for j in ORDER]

    mark, gate = routed(1, (0, 0, 0, 0))
    prepare(0, places_of(mark), gate)
    inputs[0].wait()
    inputs[1].wait()
    pack_single(0, 0, 0)

    pl.semaphore_wait(barrier, len(friends))

    def gather(i, step):
        buf = (xsg, xf)[i]
        copies = []
        for way in range(2):
            src, dst = ((NY - step + 1) % NY, NY - step) if way == 0 else (step - 1, step)
            if step < 4:
                a, b = buf.at[src], buf.at[dst]
            else:
                cut = pl.ds(way * TOK, TOK)
                a, b = buf.at[src, cut], buf.at[dst, cut]
            copies.append(start(send(a, b, gs.at[i, step - 1, way], gr.at[i, step - 1, way], ydev(1 - 2 * way))))
        return copies

    for k in (1, 7, 2, 6, 3, 5, 4):
        start(send(metas.at[0], metas.at[NY - k], ms.at[k], mr.at[NY - k], ydev(k)))
    g = {0: gather(0, 1)}

    gx = {0: send_single(0, 0)}
    inputs[2].wait()
    inputs[3].wait()
    g[1] = gather(1, 1)

    def order(width):
        m, a = iota((640, 640), 1), iota((640, 640), 0)
        i = div(a, 8 * width)
        a = a - i * 8 * width
        tensor = div(a, 4 * width)
        a = a - tensor * 4 * width
        j = div(a, width // 2)
        a = a - j * (width // 2)
        return jnp.where(m == j * 80 + i * width + tensor * (width // 2) + a, 1.0, 0.0).astype(BF)

    undo[...] = order(20)

    for k in range(1, NY):
        send(metas.at[0], metas.at[k], ms.at[k], mr.at[k], ydev(k)).wait_recv()

    sets = [(1, (u, u, v, v)) for u, v in PAIRS] + [(1, (4, 4, 4, 4))]
    sets += [(t, tuple(range(4 * h, 4 * h + 4))) for t in range(2) for h in range(2)]
    found = [routed(*one) for one in sets]
    place = places_of(jnp.concatenate([one[0] for one in found], axis=0))
    places = [place[n * NQ : (n + 1) * NQ] for n in range(8)]
    gated = [one[1] for one in found]

    def dispatch(n):
        @pl.loop(0, 2)
        def _(h):
            stack = [
                xsg[d, :, pl.ds(pl.multiple_of(i * 512 + h * 256, 256), 256)]
                for i in range(4) for d in PAIRS[n - 1]
            ]
            v = dot(big[n], jnp.concatenate(stack, axis=0)) * scale[n, :, 0:1]
            v = v.astype(BF).reshape(NQ, 80, 256)
            grecv[n - 1, 0, :, tile(h, 256)] = v[0]
            gsend[n - 1, 1:, :, tile(h, 256)] = v[1:]

        return [
            start(send(gsend.at[n - 1, j], grecv.at[n - 1, j], xs.at[n, j], xr.at[n, j], qdev(j))) for j in ORDER
        ]

    def forward(step):
        arrive(g[1])
        g[1] = gather(1, step)

    wide = NY * TOK

    def full(v, t):
        return jnp.concatenate([v[4 + 2 * t], v[5 + 2 * t]], axis=1)

    zeros = jnp.zeros((SLOT, wide), F32)

    def slots(t):
        rr, ll = iota((SLOT, wide), 0), iota((SLOT, wide), 1)
        block = div(rr, CAP)
        d = block
        if t == 1:
            up = div(block, 2)
            d = jnp.where(block == 2 * up, up + 1, NY - 1 - up)
            d = jnp.where(block == 6, 0, jnp.where(block == 7, 4, d))
        target = jnp.where(div(ll, TOK) == d, rr - block * CAP, -2).astype(F32)
        ones, lefts, rights = [], [], []
        spot, gate = full(places, t), full(gated, t)
        for j in range(NQ):
            hit = jnp.where(spot[j : j + 1, :] == target, 1.0, 0.0)
            weight = hit * gate[j : j + 1, :] if t == 0 else hit
            ones.append(hit)
            lefts += [weight, zeros]
            rights += [zeros, weight]
        if t == 0:
            pack[...] = jnp.concatenate(ones, axis=0).astype(BF)
        comb[t, 0] = jnp.concatenate(lefts, axis=0).T.astype(BF)
        comb[t, 1] = jnp.concatenate(rights, axis=0).T.astype(BF)

    def hidden(n):
        @pl.loop(0, HID // 256)
        def _(k):
            v = dot(rows[n], w[:, tile(k, 256)])
            h, a = v[0:80], v[80:160]
            s = jax.nn.sigmoid(h)
            hg = a * s * (1.0 + h * (1.0 - s))
            pair[n, :, tile(k, 256)] = jnp.concatenate([hg, h * s], axis=0).astype(BF)

    def receive(n):
        arrive(gx[n])

        @pl.loop(0, 2)
        def _(h):
            v = dot(undo[...], grecv[n - 1, :, :, tile(h, 256)].reshape(640, 256)).astype(BF)
            for i in range(4):
                rows[n - 1, :, pl.ds(pl.multiple_of(i * 512 + h * 256, 256), 256)] = v[i * 160 : (i + 1) * 160]

        hidden(n - 1)

    def forward_rows():
        @pl.loop(0, WIDE // 256)
        def _(n):
            at = tile(n, 256)
            top = dot(pack[...], xf[:, 0:TOK, at].reshape(wide, 256))
            low = dot(pack[...], xf[:, TOK : 2 * TOK, at].reshape(wide, 256))
            for j in range(NQ):
                cut = slice(j * SLOT, (j + 1) * SLOT)
                msg = jnp.concatenate([top[cut], low[cut]], axis=0).astype(BF)
                if j == 0:
                    frecv[0, :, at] = msg
                else:
                    fsend[j, :, at] = msg

        return [start(send(fsend.at[j], frecv.at[j], xs.at[5, j], xr.at[5, j], qdev(j))) for j in ORDER]

    for n in range(1, 5):
        prepare(n, places[n - 1], gated[n - 1])
        arrive(g[0])
        if n < 4:
            g[0] = gather(0, n + 1)
            gx[n] = dispatch(n)
            forward(n + 1)
        else:
            pack_single(4, 4, 1)
            gx[4] = send_single(4, 1)
        if n == 1:
            slots(0)
            undo1[...] = order(10)
            slots(1)
            w_copy.wait()
        elif n == 2:
            arrive(gx[0])
            first[...] = dot(undo1[...], orecv[0].reshape(640, 256))
            receive(1)
        else:
            receive(n - 1)

    arrive(g[1])
    fx = forward_rows()
    arrive(gx[4])
    last = dot(undo1[...], orecv[1].reshape(640, 256))
    for i in range(8):
        pieces = [v[i * 80 + h : i * 80 + h + 40] for h in (0, 40) for v in (first, last)]
        rows[3, :, i * 256 : (i + 1) * 256] = jnp.concatenate(pieces, axis=0).astype(BF)
    hidden(3)

    per = WIDE // PIECES

    def weight_part(owner, k):
        at = pl.ds(pl.multiple_of(owner * WIDE + k * per, per), per)
        return dot_tl(rows[:, :, at].reshape(640, per), pair[...].reshape(640, HID)).astype(BF)

    wcopies = []

    def other_half(k):
        wsend[k] = weight_part(1 - half, k)
        wcopies.append(start(send(wsend.at[k], wrecv.at[k], ds_.at[k], dr.at[k], {"dp": 1 - half})))

    other_half(0)
    def give_back(t, source):
        copies = []
        for h in range(2):
            unit = 2 * t + h

            @pl.loop(0, 2)
            def _(n):
                at = tile(n, 256)
                left = dot_t(source, w[pl.ds(pl.multiple_of(h * 512 + n * 256, 256), 256), :])
                right = dot_t(source, w[pl.ds(pl.multiple_of(WIDE + h * 512 + n * 256, 256), 256), :])
                for j in range(NQ):
                    cut = slice(j * SLOT, (j + 1) * SLOT)
                    msg = jnp.concatenate([left[cut], right[cut]], axis=0).astype(BF)
                    if j == 0:
                        rrecv[unit, 0, :, at] = msg
                    else:
                        rsend[unit, j, :, at] = msg

            copies.append([
                start(send(rsend.at[unit, j], rrecv.at[unit, j], bs.at[unit, j], br.at[unit, j], qdev(j)))
                for j in ORDER
            ])
        return copies

    a = iota((320, 320), 0)
    j8 = div(a, 40)
    a = a - j8 * 40
    n4 = div(a, 10)
    a = a - n4 * 10
    b2 = div(a, CAP)
    source = jnp.where(n4 < 3, n4 * 80 + j8 * 10 + a, 240 + b2 * 40 + j8 * CAP + (a - b2 * CAP))
    turn = jnp.where(iota((320, 320), 1) == source, 1.0, 0.0).astype(BF)
    b1 = give_back(1, dot(turn, pair[:, 0:80, :].reshape(320, HID)).astype(BF))

    for k in range(1, 3):
        other_half(k)

    arrive(fx)

    @pl.loop(0, WIDE // 256)
    def _(n):
        v = frecv[:, :, tile(n, 256)].astype(F32)
        frow[:, tile(n, 256)] = v[:, 0:SLOT].reshape(SLOT * NQ, 256).astype(BF)
        frow[:, pl.ds(pl.multiple_of(WIDE + n * 256, 256), 256)] = v[:, SLOT:].reshape(SLOT * NQ, 256).astype(BF)

    @pl.loop(0, HID // 256)
    def _(n):
        h = dot(frow[...], w[:, tile(n, 256)])
        fh[:, tile(n, 256)] = (h * jax.nn.sigmoid(h)).astype(BF)

    b0 = give_back(0, fh[...])
    for k in range(3, 4):
        other_half(k)

    def combine(u):
        @pl.loop(0, 2)
        def _(n):
            at = tile(n, 256)
            got = rrecv[u, :, :, at].reshape(2 * SLOT * NQ, 256)
            part[u, :, 0:TOK, at] = dot(comb[u // 2, 0], got).reshape(NY, TOK, 256)
            part[u, :, TOK : 2 * TOK, at] = dot(comb[u // 2, 1], got).reshape(NY, TOK, 256)

    r = {}

    def reduce_step(u, step):
        copies = []
        for way in range(2):
            if step == 1:
                cut = slice(way * TOK, (way + 1) * TOK)
                ysend[u, 0, way, cut] = part[u, 4, cut].astype(BF)
                where = pl.ds(way * TOK, TOK)
                a, b = ysend.at[u, 0, way, where], yrecv.at[u, 0, way, where]
            else:
                s = step - 1
                r[u][way].wait_recv()
                d = 5 - step if way == 0 else 3 + step
                if step == 2:
                    got = slice(way * TOK, (way + 1) * TOK)
                    rest = slice((1 - way) * TOK, (2 - way) * TOK)
                    ysend[u, s, way, got] = (part[u, d, got] + yrecv[u, 0, way, got].astype(F32)).astype(BF)
                    ysend[u, s, way, rest] = part[u, d, rest].astype(BF)
                else:
                    ysend[u, s, way] = (part[u, d] + yrecv[u, s - 1, way].astype(F32)).astype(BF)
                a, b = ysend.at[u, s, way], yrecv.at[u, s, way]
            copies.append(start(send(a, b, ys.at[u, step - 1, way], yr.at[u, step - 1, way], ydev(1 - 2 * way))))
        r[u] = copies

    pipes = {}

    def finish(u):
        arrive(r[u])
        total = part[u, 0] + yrecv[u, 3, 0].astype(F32) + yrecv[u, 3, 1].astype(F32)
        t, h = u // 2, u % 2
        for i in range(2):
            if t == 1:
                base = xsg[0, TOK : 2 * TOK, i * WIDE + h * 512 : i * WIDE + h * 512 + 512]
            else:
                base = xf[0, i * TOK : (i + 1) * TOK, h * 512 : h * 512 + 512]
            cut = slice(i * TOK, (i + 1) * TOK)
            out_send[u, cut] = (base.astype(F32) + total[cut]).astype(BF)
        to = (p + (3 if t == 1 else 1)) % 4
        pipes[u] = start(send(out_send.at[u], out_recv.at[u], ps.at[u], pr.at[u], {"pipe": to}))

    def own_half(k):
        wown[k] = weight_part(half, k)

    outs = []

    def place_out(src, dst):
        copy = pltpu.make_async_copy(src, dst, out_sem.at[len(outs)])
        copy.start()
        outs.append(copy)

    def sum_half(k):
        wcopies[k].wait_recv()
        wown[k] = (wown[k].astype(F32) + wrecv[k].astype(F32)).astype(BF)
        place_out(wown.at[k], wg_ref.at[pl.ds(k * per, per)])

    waits = {2: b1[0], 3: b1[1], 0: b0[0], 1: b0[1]}
    begun = {2: 0, 3: 2, 0: 4, 1: 6}
    pieces = list(range(PIECES))
    later = (1, 3, 5, 7)
    for tick in range(11):
        for u in (2, 3, 0, 1):
            step = tick - begun[u] + 1
            if step == 1:
                arrive(waits[u])
                combine(u)
            if 1 <= step <= 4:
                reduce_step(u, step)
            if step == 5:
                finish(u)
        for _ in range(2):
            if pieces:
                own_half(pieces.pop(0))
        if tick in later:
            other_half(4 + later.index(tick))
        if tick in (4, 6, 8, 9):
            sum_half((4, 6, 8, 9).index(tick))

    def take(u):
        pipes[u].wait_recv()
        out = prior_ref if u >= 2 else next_ref
        for i in range(2):
            place_out(out_recv.at[u, pl.ds(i * TOK, TOK)], out.at[:, pl.ds(i * WIDE + (u % 2) * 512, 512)])

    take(2)
    take(3)
    for k in range(4, PIECES):
        sum_half(k)
    take(0)
    take(1)
    for copy in outs:
        copy.wait()
    for copy in sent:
        copy.wait_send()


def finish_kernel(a, b, c, x, y, z, va, vb, vc, sems):
    pieces = [(c.at[pl.ds(i * 256, 256)], vc.at[i], z.at[pl.ds(i * 256, 256)]) for i in range(4)]
    pieces += [(a, va, x), (b, vb, y)]
    loads = [pltpu.make_async_copy(u, m, sems.at[0, i]) for i, (u, m, _) in enumerate(pieces)]
    stores = [pltpu.make_async_copy(m, o, sems.at[1, i]) for i, (_, m, o) in enumerate(pieces)]
    for copy in loads:
        copy.start()
    for load, store in zip(loads, stores):
        load.wait()
        store.start()
    for copy in stores:
        copy.wait()


def relay(rf, rb, gf, gb, s, o, f, w):
    vmem = pl.BlockSpec(memory_space=pltpu.VMEM)
    dma = pltpu.SemaphoreType.DMA
    v = pltpu.VMEM
    two = 2 * SLOT
    return pl.pallas_call(
        kernel,
        out_shape=(
            jax.ShapeDtypeStruct((TOK, D), BF),
            jax.ShapeDtypeStruct((TOK, D), BF),
            jax.ShapeDtypeStruct((D // 2, HID), BF),
        ),
        in_specs=[vmem] * 4 + [pl.BlockSpec(memory_space=pl.ANY)] * 4,
        out_specs=(pl.BlockSpec(memory_space=pl.ANY),) * 3,
        scratch_shapes=[
            v((D, HID), BF),
            v((NY, 8, 128), F32),
            v((NY, 2 * TOK, D), BF),
            v((NY, 2 * TOK, WIDE), BF),
            v((3, NQ, two, 512), BF),
            v((3, NQ, two, 512), BF),
            v((2, NQ, two, 256), BF),
            v((2, NQ, two, 256), BF),
            v((640, 256), F32),
            v((NQ, two, WIDE), BF),
            v((NQ, two, WIDE), BF),
            v((4, NQ, two, 512), BF),
            v((4, NQ, two, 512), BF),
            v((4, 160, D), BF),
            v((4, 160, HID), BF),
            v((SLOT * NQ, D), BF),
            v((SLOT * NQ, HID), BF),
            v((5, 640, 512), BF),
            v((5, 640, 128), F32),
            v((640, 640), BF),
            v((640, 640), BF),
            v((SLOT * NQ, NY * TOK), BF),
            v((2, 2, NY * TOK, two * NQ), BF),
            v((4, NY, 2 * TOK, 512), F32),
            v((4, 4, 2, 2 * TOK, 512), BF),
            v((4, 4, 2, 2 * TOK, 512), BF),
            v((4, 2 * TOK, 512), BF),
            v((4, 2 * TOK, 512), BF),
            v((PIECES, WIDE // PIECES, HID), BF),
            v((PIECES, WIDE // PIECES, HID), BF),
            v((PIECES, WIDE // PIECES, HID), BF),
            dma,
            dma((4,)),
            dma((PIECES + 8,)),
            dma((NY,)), dma((NY,)),
            dma((2, 4, 2)), dma((2, 4, 2)),
            dma((6, NQ)), dma((6, NQ)),
            dma((4, NQ)), dma((4, NQ)),
            dma((4, 4, 2)), dma((4, 4, 2)),
            dma((PIECES,)), dma((PIECES,)),
            dma((4,)), dma((4,)),
        ],
        compiler_params=pltpu.CompilerParams(
            collective_id=0, has_side_effects=True, vmem_limit_bytes=58 << 20
        ),
        cost_estimate=pl.CostEstimate(flops=8 * 10**9, bytes_accessed=10**7, transcendentals=10**6),
        name="relay",
    )(rf, rb, gf, gb, s, o, f, w)


def on_device(section_inputs, saved_inputs, output_grads, forward_routes, backward_routes,
              forward_gates, backward_gates, expert_weights):
    outs = relay(
        forward_routes[0].T, backward_routes[0].T, forward_gates[0].T, backward_gates[0].T,
        saved_inputs[0], output_grads[0], section_inputs[0], expert_weights[0, 0],
    )
    anywhere = pl.BlockSpec(memory_space=pl.ANY)
    after, prior, wg = pl.pallas_call(
        finish_kernel,
        out_shape=[jax.ShapeDtypeStruct(v.shape, v.dtype) for v in outs],
        in_specs=[anywhere] * 3,
        out_specs=[anywhere] * 3,
        scratch_shapes=[
            pltpu.VMEM((TOK, D), BF),
            pltpu.VMEM((TOK, D), BF),
            pltpu.VMEM((4, 256, HID), BF),
            pltpu.SemaphoreType.DMA((2, 6)),
        ],
        name="place",
    )(*outs)
    return after[None], prior[None], wg[None, None]


def solution(mesh):
    placed = P("pipe", ("expert", "dp"), None)
    return jax.shard_map(
        on_device,
        mesh=mesh,
        in_specs=(placed,) * 7 + (P("pipe", "expert", None, None),),
        out_specs=(placed, placed, P("pipe", "expert", "dp", None)),
        check_vma=False,
    )
```
